256 devices in a mesh: ka: 64 (over x, z, y_lo), ga: 4 (over y_hi, core).
Axes of the slice: x: 4, y: 4 (y_hi: 2, y_lo: 2; y = y_hi * 2 + y_lo), z: 8, core: 2. Of those that a mesh axis runs over, the one named last changes fastest.
Arguments:
- bloch_samples: bfloat16 [384, 2, 8, 1024], P('ka'), may hold values from -6 to 6
- zeta_vectors: bfloat16 [1024, 2, 1024], P(None, None, 'ga'), may hold values from -0.01171875 to 0.01171875
- screened: bfloat16 [22, 2, 1024, 1024], P(None, None, ('ga', 'ka')), may hold values from -1 to 9, as said below
- pair_slots: int32 [384, 2, 6], P('ka'), may hold values from 0 to 21
Outputs:
- kernel: float32 [384, 4, 2, 1536], P('ka', None, None, 'ga')
The draws below stay inside these ranges and needn't reach their ends.
Inputs may be any that keep to these rules, and one draw needn't show every extreme that they name: pair_slots[k, o, j2] is the slot in the first dimension of screened used for the pair of k-point k and the j2-th k-point of the block o + 1 blocks after the block of k, blocks taken cyclically; slots may be assigned arbitrarily. Every screened[s] is Hermitian: screened[s, 0] is symmetric and screened[s, 1] antisymmetric.
All inputs are finite; a program needn't handle non-finite values.
Results may differ from the reference program's by a relative error of at most 0.0051.
Values may be sent and summed in bfloat16 or wider, within the bound.
No kernel may reach another device: no remote copies, remote signals or barrier semaphores. Data moves between devices by JAX's collectives and lax.ppermute only.
A program may use at most 128 MiB of HBM per device.

```python
from functools import partial
import jax
import jax.numpy as jnp
from jax import lax

NV = 4
NC = 4
NB = 8
NMU = 1024
NG = 1024
KB = 6
NK = 384
NQ = 22


def draw_screened(key, part):
    key = jax.random.fold_in(key, 7)
    key_off, key_diag = jax.random.split(key)
    full_shape = (NQ, 2, NG, NG)
    off_diag = jnp.clip(jax.random.normal(key_off, full_shape, jnp.float32), -6.0, 6.0)
    log_diag = jax.random.uniform(key_diag, (NQ, NG), jnp.float32, 0.0, jnp.log(4.0))
    off_diag = off_diag / jnp.sqrt(jnp.float32(NG))
    real_raw = off_diag[:, 0]
    imag_raw = off_diag[:, 1]
    real_sym = (real_raw + jnp.swapaxes(real_raw, 1, 2)) * 0.70710677
    imag_anti = (imag_raw - jnp.swapaxes(imag_raw, 1, 2)) * 0.70710677
    identity = jnp.eye(NG, dtype=jnp.float32)
    real_part = real_sym + jnp.exp(log_diag)[:, :, None] * identity[None]
    return jnp.stack([real_part, imag_anti], axis=1).astype(jnp.bfloat16)


def with_ends(entries, stream_key, least, top_value):
    place = [jax.random.randint(jax.random.fold_in(stream_key, axis), (), 0, length) for axis, length in enumerate(entries.shape)]
    longest = entries.shape.index(max(entries.shape))
    neighbour = place[:longest] + [(place[longest] + 1) % entries.shape[longest]] + place[longest + 1:]
    return entries.at[tuple(place)].set(least).at[tuple(neighbour)].set(top_value)


def steps_of(rng, shape, pieces, least, high):
    loudness, own = 1.0, jax.random.fold_in(rng, 6)
    for position, blocks in pieces:
        steps = jnp.exp(jax.random.uniform(jax.random.fold_in(own, position), (blocks,), jnp.float32, least / len(pieces), high / len(pieces)))
        loudness = loudness * jnp.repeat(steps, shape[position] // blocks).reshape([-1 if axis == position else 1 for axis in range(len(shape))])
    return loudness


def centred(rng, shape, scale, limit, cuts=(), held_as=jnp.bfloat16):
    values = jax.random.normal(rng, shape, jnp.float32) * scale
    if len(cuts) > 0:
        values = steps_of(rng, shape, cuts, -0.22, 0.18) * values
    return jnp.clip(values, min=-limit, max=limit).astype(held_as)


def setup_inputs(seed: int = 0) -> dict:
    streams_of = jax.random.split(jax.random.key(seed), 5)
    return {
        "bloch_samples": centred(streams_of[0], (NK, 2, NB, NMU), 1.0, 6.0, ((0, 64),)),
        "zeta_vectors": centred(streams_of[1], (NMU, 2, NG), (NMU * NG // 4) ** -0.5, 0.01171875, ((2, 4),)),
        "screened": draw_screened(jax.random.fold_in(streams_of[4], 71), 0),
        "pair_slots": with_ends(jax.random.randint(streams_of[3], (NK, 2, KB), 0, NQ), jax.random.fold_in(streams_of[3], 1), 0, NQ - 1).astype(jnp.int32),
    }


def pair_products(left_bands, right_bands):
    left_real = left_bands[:, 0].astype(jnp.float32)[:, None, :, None, :]
    left_imag = left_bands[:, 1].astype(jnp.float32)[:, None, :, None, :]
    right_real = right_bands[:, 0].astype(jnp.float32)[None, :, None, :, :]
    right_imag = right_bands[:, 1].astype(jnp.float32)[None, :, None, :, :]
    real_part = left_real * right_real + left_imag * right_imag
    imag_part = left_real * right_imag - left_imag * right_real
    return real_part.astype(jnp.bfloat16), imag_part.astype(jnp.bfloat16)


def densities(real_part, imag_part, zeta_vectors):
    points = zeta_vectors.shape[0]
    flat_real = real_part.reshape(-1, points)
    flat_imag = imag_part.reshape(-1, points)
    vector_real = zeta_vectors[:, 0]
    vector_imag = zeta_vectors[:, 1]
    density_real = jnp.dot(flat_real, vector_real, preferred_element_type=jnp.float32) - jnp.dot(flat_imag, vector_imag, preferred_element_type=jnp.float32)
    density_imag = jnp.dot(flat_real, vector_imag, preferred_element_type=jnp.float32) + jnp.dot(flat_imag, vector_real, preferred_element_type=jnp.float32)
    return density_real.astype(jnp.bfloat16), density_imag.astype(jnp.bfloat16)


def screen_pair(screened, pair_items):
    slot_index, valence_real, valence_imag, conduction_real, conduction_imag = pair_items
    matrix = lax.dynamic_index_in_dim(screened, slot_index, 0, keepdims=False).reshape(2 * NG, NG)
    stacked = jnp.concatenate([valence_real, valence_imag], axis=0)
    applied = jnp.dot(matrix, stacked.T, preferred_element_type=jnp.float32)
    band_pairs = NV * NV
    upper_rows = applied[:NG]
    lower_rows = applied[NG:]
    screened_real = upper_rows[:, :band_pairs] - lower_rows[:, band_pairs:]
    screened_imag = upper_rows[:, band_pairs:] + lower_rows[:, :band_pairs]
    highest = lax.Precision.HIGHEST
    left_real = conduction_real.astype(jnp.float32)
    left_imag = conduction_imag.astype(jnp.float32)
    kernel_real = jnp.dot(left_real, screened_real, precision=highest) + jnp.dot(left_imag, screened_imag, precision=highest)
    kernel_imag = jnp.dot(left_real, screened_imag, precision=highest) - jnp.dot(left_imag, screened_real, precision=highest)
    return jnp.stack([kernel_real, kernel_imag])


def arranged(values, block_points):
    shaped = values.reshape(2, block_points, block_points, 2, NC, NC, NV, NV)
    length = block_points * NV * NC * NV * NC
    own_rows = jnp.transpose(shaped, (1, 0, 3, 2, 6, 4, 7, 5)).reshape(block_points, 2, 2, length)
    mirror = jnp.transpose(shaped, (2, 0, 3, 1, 7, 5, 6, 4)).reshape(block_points, 2, 2, length)
    mirror = mirror * jnp.array([1.0, -1.0], dtype=jnp.float32).reshape(1, 1, 2, 1)
    return own_rows, mirror


def reference(bloch_samples, zeta_vectors, screened, pair_slots):
    blocks = NK // KB

    def one_block(block_index):
        own_bands = lax.dynamic_slice_in_dim(bloch_samples, block_index * KB, KB, 0)
        slots_here = lax.dynamic_slice_in_dim(pair_slots, block_index * KB, KB, 0)
        results = []
        for offset in (1, 2):
            partner_start = (((block_index + offset) % blocks) * KB).astype(jnp.int32)
            partner = lax.dynamic_slice_in_dim(bloch_samples, partner_start, KB, 0)
            cond_real, cond_imag = pair_products(own_bands[:, :, NV:], partner[:, :, NV:])
            val_real, val_imag = pair_products(own_bands[:, :, :NV], partner[:, :, :NV])
            cond_dreal, cond_dimag = densities(cond_real, cond_imag, zeta_vectors)
            val_dreal, val_dimag = densities(val_real, val_imag, zeta_vectors)
            pair_items = (
                slots_here[:, offset - 1].reshape(-1).astype(jnp.int32),
                val_dreal.reshape(KB * KB, NV * NV, NG),
                val_dimag.reshape(KB * KB, NV * NV, NG),
                cond_dreal.reshape(KB * KB, NC * NC, NG),
                cond_dimag.reshape(KB * KB, NC * NC, NG),
            )
            results.append(lax.map(partial(screen_pair, screened), pair_items))
        direct = jnp.stack(results)
        return arranged(direct, KB)

    own_all, mirror_all = lax.map(one_block, jnp.arange(blocks, dtype=jnp.int32))
    length = KB * NV * NC * NV * NC
    own_rows = own_all.reshape(NK, 2, 2, length)
    first_back = jnp.roll(mirror_all[:, :, 0], 1, axis=0).reshape(NK, 1, 2, length)
    second_back = jnp.roll(mirror_all[:, :, 1], 2, axis=0).reshape(NK, 1, 2, length)
    return jnp.concatenate([own_rows, first_back, second_back], axis=1)
```

```python
import functools
import jax
import jax.numpy as jnp
from jax import lax
from jax.experimental import pallas as pl
from jax.experimental.pallas import tpu as pltpu
from jax.sharding import PartitionSpec as P

f32 = jnp.float32
bf16 = jnp.bfloat16

WIN = 8
KB = 6
PAIRS = 72
TOTAL = WIN * PAIRS
CHUNK = 16
SLOTS = 22
CHUNKS = (TOTAL + SLOTS * (CHUNK - 1)) // CHUNK // 2 * 2 + 2
MSG = 112
VMEM_LIMIT = 50 * 1024 * 1024


def from_behind(x, axis, by):
    count = lax.axis_size(axis)
    return lax.ppermute(x, axis, [(i, (i + by) % count) for i in range(count)])


def half_swap(mask, first, second):
    return jnp.where(mask, first, pltpu.roll(second, 4, 0))


def density_kernel(near_ref, far_ref, zv_ref, zc_ref, *rest):
    mv_ref, mc_ref, left, right, va, ca, vb, cb = rest[-8:]
    step = pl.program_id(0)
    low = lax.broadcasted_iota(jnp.int32, (8, 1024), 0) < 4

    def produce(chunk, v_buf, c_buf):
        block = chunk // 3
        jh = chunk % 3
        for cv, buf in ((0, v_buf), (1, c_buf)):
            for jl in range(2):
                point = block * KB + 2 * jh + jl
                for part in range(4):
                    cols = slice(256 * part, 256 * part + 256)
                    imag_cols = slice(1024 + 256 * part, 1280 + 256 * part)
                    lefts = []
                    for band in range(4):
                        row = 4 * cv + band
                        lr = jnp.broadcast_to(left[point, row : row + 1, cols], (8, 256))
                        li = jnp.broadcast_to(left[point, 8 + row : 9 + row, cols], (8, 256))
                        lefts.append((lr, li))
                    for o in range(2):
                        for p in range(3):
                            rr = right[(block + o) * 3 + p, cv, 0, :, cols]
                            ri = right[(block + o) * 3 + p, cv, 1, :, cols]
                            base = ((jl * 2 + o) * 3 + p) * 32
                            for half in range(2):
                                reals = []
                                imags = []
                                for lr, li in lefts[2 * half : 2 * half + 2]:
                                    reals.append(lr * rr + li * ri)
                                    imags.append(lr * ri - li * rr)
                                rows = slice(base + 16 * half, base + 16 * half + 16)
                                buf[rows, cols] = jnp.concatenate(reals, axis=0).astype(bf16)
                                buf[rows, imag_cols] = jnp.concatenate(imags, axis=0).astype(bf16)
                    yield

    def consume(sub, v_buf, c_buf):
        mask = lax.broadcasted_iota(jnp.int32, (8, 256), 0) < 4
        for buf, z_ref, out_ref in ((v_buf, zv_ref, mv_ref), (c_buf, zc_ref, mc_ref)):
            for tile in range(z_ref.shape[1] // 256):
                cols = slice(256 * tile, 256 * tile + 256)
                for jl in range(2):
                    res = jnp.dot(buf[192 * jl : 192 * jl + 192], z_ref[:, cols], preferred_element_type=f32)
                    for o in range(2):
                        for p in range(3):
                            base = (o * 3 + p) * 32
                            a = [res[base + 8 * c : base + 8 * c + 8] for c in range(4)]
                            first = [half_swap(mask, a[0], a[1]), half_swap(mask, a[2], a[3])]
                            second = [
                                jnp.where(mask, pltpu.roll(a[0], 4, 0), a[1]),
                                jnp.where(mask, pltpu.roll(a[2], 4, 0), a[3]),
                            ]
                            for jj, value in ((0, first), (1, second)):
                                index = sub * 24 + (2 * p + jj) * 4 + jl * 2 + o
                                out_ref[index, :, cols] = jnp.concatenate(value, axis=0).astype(bf16)
                    yield

    def drain(*generators):
        live = list(generators)
        while live:
            live = [g for g in live if next(g, True) is None]

    @pl.when(step == 0)
    def _():
        for b in range(4):
            ref = near_ref if b < 2 else far_ref
            for j in range(KB):
                x = ref[b % 2, 16 * j : 16 * j + 16, :].astype(f32)
                if b < 2:
                    left[b * KB + j] = x
                if b > 0:
                    p = j // 2
                    for r in range(2):
                        half = x[8 * r : 8 * r + 8]
                        if j % 2 == 0:
                            right[(b - 1) * 3 + p, 0, r] = half
                            right[(b - 1) * 3 + p, 1, r] = pltpu.roll(half, 4, 0)
                        else:
                            index = (b - 1) * 3 + p
                            right[index, 0, r] = jnp.where(low, right[index, 0, r], pltpu.roll(half, 4, 0))
                            right[index, 1, r] = jnp.where(low, right[index, 1, r], half)
        drain(produce(0, va, ca))

    drain(consume(0, va, ca), produce(2 * step + 1, vb, cb))
    drain(consume(1, vb, cb), produce(jnp.minimum(2 * step + 2, 5), va, ca))


def densities(call, near, far, zv, zc, previous):
    whole = lambda shape: pl.BlockSpec(shape, lambda n: (0,) * len(shape), pipeline_mode=pl.Buffered(1))
    in_specs = [whole(near.shape), whole(far.shape), whole(zv.shape), whole(zc.shape)]
    operands = [near, far, zv, zc]
    aliases = {}
    if previous is not None:
        in_specs += [pl.BlockSpec(memory_space=pl.ANY)] * 2
        operands += list(previous)
        aliases = {4: 0, 5: 1}
    wv = zv.shape[1]
    wc = zc.shape[1]
    flops = 2 * 2 * PAIRS * 16 * 2048 * (wv + wc)
    return pl.pallas_call(
        density_kernel,
        grid=(3,),
        in_specs=in_specs,
        out_specs=[
            pl.BlockSpec((48, 16, wv), lambda n: (3 * call + n, 0, 0)),
            pl.BlockSpec((48, 16, wc), lambda n: (3 * call + n, 0, 0)),
        ],
        out_shape=[
            jax.ShapeDtypeStruct((TOTAL, 16, wv), bf16),
            jax.ShapeDtypeStruct((TOTAL, 16, wc), bf16),
        ],
        scratch_shapes=[
            pltpu.VMEM((2 * KB, 16, 1024), f32),
            pltpu.VMEM((9, 2, 2, 8, 1024), f32),
            pltpu.VMEM((384, 2048), bf16),
            pltpu.VMEM((384, 2048), bf16),
            pltpu.VMEM((384, 2048), bf16),
            pltpu.VMEM((384, 2048), bf16),
        ],
        input_output_aliases=aliases,
        compiler_params=pltpu.CompilerParams(vmem_limit_bytes=VMEM_LIMIT),
        cost_estimate=pl.CostEstimate(flops=flops, bytes_accessed=8 * 2**20, transcendentals=0),
        name="densities",
    )(*operands)


def quarter_rows():
    own = [[(0, 0, 0, 16)], [(0, 16, 0, 8), (1, 0, 8, 8)], [(1, 8, 0, 16)]]
    own += [[(q + 2, r, s, n) for q, r, s, n in item] for item in own]
    mirror = [[(0, 24)], [(0, 40), (1, 24)], [(1, 40)]]
    mirror += [[(q + 2, r) for q, r in item] for item in mirror]
    return own, mirror


def apply_kernel(order_ref, slot_ref, used_ref, ga_ref, mv_ref, mc_ref, w_ref, out_ref, rhs, xv):
    ga = ga_ref[0]
    lane_group = lax.broadcasted_iota(jnp.int32, (16, 128), 1) >> 5
    spots = [(((q & 1) ^ (ga & 1)) << 1) | ((q >> 1) ^ (ga >> 1)) for q in range(4)]
    own_rows, mirror_rows = quarter_rows()

    def build(slot, carry):
        for x in range(4):
            wr = w_ref[x, slot, 0]
            wi = w_ref[x, slot, 1]
            rhs[slot, 64 * x : 64 * x + 64, 0:128] = wr
            rhs[slot, 64 * x : 64 * x + 64, 128:256] = -wi
            rhs[slot, 256 + 64 * x : 320 + 64 * x, 0:128] = wi
            rhs[slot, 256 + 64 * x : 320 + 64 * x, 128:256] = wr
        return carry

    lax.fori_loop(0, SLOTS, build, 0)

    def chunk(q, carry):
        for u in range(2):
            slot = slot_ref[2 * q + u]
            ids = [order_ref[(2 * q + u) * CHUNK + i] for i in range(CHUNK)]
            sources = [jnp.minimum(i, TOTAL - 1) for i in ids]
            lhs = jnp.concatenate([mv_ref[s] for s in sources], axis=0)
            res = jnp.dot(lhs, rhs[slot], preferred_element_type=f32).astype(bf16)
            for i in range(CHUNK):
                xv[ids[i]] = res[16 * i : 16 * i + 16]
        return carry

    lax.fori_loop(0, (used_ref[0] + 1) >> 1, chunk, 0)

    def contract(t, carry):
        for jh in range(3):
            for h in range(3):
                first = ((t * 3 + jh) * 6 + 2 * h) * 4
                rows = []
                for i in range(8):
                    y = mc_ref[first + i]
                    rows.append(y)
                    rows.append(jnp.concatenate([-y[:, 128:], y[:, :128]], axis=1))
                lhs = jnp.concatenate([xv[first + i] for i in range(8)], axis=0)
                d = lax.dot_general(
                    lhs, jnp.concatenate(rows, axis=0), (((1,), (1,)), ((), ())), preferred_element_type=f32
                )
                blocks = [
                    [d[16 * i : 16 * i + 16, 128 * (i // 4) : 128 * (i // 4) + 128] for i in range(4 * l, 4 * l + 4)]
                    for l in range(2)
                ]
                odd = (lane_group & 1) == 1
                low = lane_group < 2
                mixed = [[jnp.where(odd, b[2 * jl + 1], b[2 * jl]) for jl in range(2)] for b in blocks]
                for l in range(2):
                    own = jnp.where(low, mixed[l][0], mixed[l][1])
                    for q, r, s, n in own_rows[2 * h + l]:
                        out_ref[spots[q], t, jh, r : r + n, :] = own[s : s + n]
                for jl in range(2):
                    if jl == 0:
                        mirror = jnp.where(low, mixed[0][0], pltpu.roll(mixed[1][0], 64, 1))
                    else:
                        mirror = jnp.where(low, pltpu.roll(mixed[0][1], 64, 1), mixed[1][1])
                    for q, r in mirror_rows[2 * jh + jl]:
                        out_ref[spots[q], t, h, r : r + 16, :] = mirror
        return carry

    lax.fori_loop(0, WIN, contract, 0)


def apply_screened(order, slots, used, ga, mv, mc, w):
    smem = pl.BlockSpec(memory_space=pltpu.SMEM)
    vmem = pl.BlockSpec(memory_space=pltpu.VMEM)
    return pl.pallas_call(
        apply_kernel,
        in_specs=[smem] * 4 + [vmem] * 3,
        out_specs=vmem,
        out_shape=jax.ShapeDtypeStruct((4, WIN, 3, 56, 128), f32),
        scratch_shapes=[
            pltpu.VMEM((SLOTS, 512, 256), bf16),
            pltpu.VMEM((TOTAL + 1, 16, 256), bf16),
        ],
        compiler_params=pltpu.CompilerParams(vmem_limit_bytes=VMEM_LIMIT),
        cost_estimate=pl.CostEstimate(flops=6 * 10**9, bytes_accessed=18 * 2**20, transcendentals=0),
        name="apply_screened",
    )(order, slots, used, ga, mv, mc, w)


def split_dot(x, sel):
    high = x.astype(bf16)
    low = (x - high.astype(f32)).astype(bf16)
    return jnp.dot(high, sel, preferred_element_type=f32) + jnp.dot(low, sel, preferred_element_type=f32)


def arrange_kernel(ga_ref, parts_ref, out_ref):
    ga = ga_ref[0]
    src = lax.broadcasted_iota(jnp.int32, (128, 384), 0)
    lane = lax.broadcasted_iota(jnp.int32, (128, 384), 1)
    row = lax.broadcasted_iota(jnp.int32, (32, 384), 0)
    row_lane = lax.broadcasted_iota(jnp.int32, (32, 384), 1)
    start = ga + (ga >> 1)
    outer = row_lane >> 6
    place = 6 * ga + outer
    own = (24, (lane >> 4) & 3, lane & 3, outer * 4 + ((row_lane >> 2) & 3))
    mirror = (32, lane & 3, (lane >> 4) & 3, ((place >> 2) - start) * 16 + ((row_lane >> 2) & 3) * 4 + (place & 3))
    for kind, (count, c, c2, wanted) in enumerate((own, mirror)):
        low = 24 * kind
        x = jnp.concatenate([parts_ref[jh, low : low + count, :] for jh in range(3)], axis=0)
        keep = row[:count] == wanted[:count]
        for combo in range(8):
            sel = (src == combo * 16 + c * 4 + c2).astype(f32).astype(bf16)
            spread = split_dot(x, sel)
            for jh in range(3):
                rows = spread[count * jh : count * jh + count]
                picked = jnp.sum(jnp.where(keep, rows, 0.0), axis=0, keepdims=True)
                if kind == 1 and combo % 2 == 1:
                    picked = -picked
                out_ref[2 * jh + combo // 4, 2 * kind + (combo // 2) % 2, pl.ds(combo % 2, 1), :] = picked


def arrange(ga, parts):
    vmem = pl.BlockSpec(memory_space=pltpu.VMEM)
    return pl.pallas_call(
        arrange_kernel,
        in_specs=[pl.BlockSpec(memory_space=pltpu.SMEM), vmem],
        out_specs=vmem,
        out_shape=jax.ShapeDtypeStruct((KB, 4, 2, 384), f32),
        compiler_params=pltpu.CompilerParams(vmem_limit_bytes=VMEM_LIMIT),
        name="arrange",
    )(ga, parts)


def schedule(slots):
    pair = jnp.arange(TOTAL, dtype=jnp.int32)
    names = jnp.arange(SLOTS, dtype=jnp.int32)
    hot = slots[:, None] == names[None, :]
    needed = (jnp.sum(hot.astype(jnp.int32), axis=0) + CHUNK - 1) // CHUNK
    start = jnp.sum(jnp.where(names[:, None] < names[None, :], needed[:, None], 0), axis=0)
    same = (slots[:, None] == slots[None, :]) & (pair[None, :] < pair[:, None])
    rank = jnp.sum(same.astype(jnp.int32), axis=1)
    place = jnp.sum(jnp.where(hot, start[None, :], 0), axis=1) * CHUNK + rank
    seat = jnp.arange(CHUNKS * CHUNK, dtype=jnp.int32)
    taken = place[None, :] == seat[:, None]
    order = TOTAL + jnp.sum(jnp.where(taken, pair[None, :] - TOTAL, 0), axis=1)
    chunk = jnp.arange(CHUNKS, dtype=jnp.int32)
    ended = (start + needed)[None, :] <= chunk[:, None]
    slot_of = jnp.minimum(jnp.sum(ended.astype(jnp.int32), axis=1), SLOTS - 1)
    return order, slot_of, jnp.sum(needed).reshape(1)


def zeta_matrix(zeta):
    zr = zeta[:, 0]
    zi = zeta[:, 1]
    return jnp.concatenate([jnp.concatenate([zr, zi], axis=1), jnp.concatenate([-zi, zr], axis=1)], axis=0)


def body(bloch_samples, zeta_vectors, screened, pair_slots):
    ka_count = lax.axis_size("ka")
    ka = lax.axis_index("ka")
    ga = lax.axis_index("ga")
    ga_word = ga.reshape(1).astype(jnp.int32)
    part = lax.rem(ka, WIN)
    slots = jnp.transpose(pair_slots.reshape(3, 2, 2, KB), (0, 3, 1, 2)).reshape(1, PAIRS)
    tail = jnp.pad(slots.astype(bf16), ((0, 15), (0, 1024 - PAIRS)))
    message = jnp.concatenate([bloch_samples.reshape(96, 1024), tail], axis=0)
    following = from_behind(message, "ka", -1)
    pieces = jnp.transpose(screened.reshape(SLOTS, 2, 4, WIN, 128), (3, 0, 1, 2, 4))
    pieces = jnp.concatenate([pieces, pieces], axis=0)
    line = 2 * WIN
    near_groups = [[x * line + s for s in range(line)] for x in range(ka_count // line)]
    x_groups = [[x * line + s for x in range(ka_count // line)] for s in range(line)]
    pieces = lax.all_to_all(pieces, "ka", 0, 0, axis_index_groups=near_groups, tiled=True)
    rows = jnp.transpose(pieces, (1, 2, 0, 3, 4)).reshape(SLOTS, 2, 4 * line, 128)
    w = lax.all_gather(rows, "ka", axis_index_groups=x_groups)
    zv = zeta_matrix(zeta_vectors)
    mine = lax.dynamic_slice_in_dim(zeta_vectors, 128 * lax.rem(part, 2), 128, 2)
    mine, following = lax.optimization_barrier((mine, following))
    holders = [(k, (k % WIN) // 2) for k in range(ka_count)]
    over = lax.ppermute(mine, ("ka", "ga"), [(4 * k + h, 4 * k + (h ^ 2)) for k, h in holders])
    held = jnp.where(ga == part // 2, mine, over)
    moves = [(4 * k + h, 4 * k + (h ^ 1)) for k, h in holders]
    moves += [(4 * k + (h ^ 2), 4 * k + (h ^ 3)) for k, h in holders]
    zc = zeta_matrix(held + lax.ppermute(held, ("ka", "ga"), moves))
    here = jnp.stack([message, following])
    ahead = from_behind(here, "ka", -2)
    behind = from_behind(here, "ka", 2)
    ahead2 = from_behind(ahead, "ka", -2)
    behind2 = from_behind(behind, "ka", 2)
    pairs = [behind2, behind, here, ahead, ahead2]
    made = None
    for call in (2, 1, 3, 0):
        made = densities(call, pairs[call], pairs[call + 1], zv, zc, made)
    mv, mc = made
    all_slots = jnp.concatenate([x[:, 96, :PAIRS] for x in pairs[:4]], axis=0).reshape(TOTAL)
    order, slot_of, used = schedule(all_slots.astype(jnp.int32))
    partial = apply_screened(order, slot_of, used, ga_word, mv, mc, w)
    arrived = lax.ppermute(partial[2:].astype(bf16), "ga", [(0, 1), (1, 0), (2, 3), (3, 2)])
    own = partial[0] + arrived[0].astype(f32)
    other = (partial[1] + arrived[1].astype(f32)).astype(bf16)
    own = own + lax.ppermute(other, "ga", [(0, 2), (2, 0), (1, 3), (3, 1)]).astype(f32)
    first_offset = ((lax.broadcasted_iota(jnp.int32, (1, 1, 1, 128), 3) >> 5) & 1) == 0
    spread = lambda x, before, after: jnp.pad(x, ((before, after), (0, 0), (0, 0), (0, 0)))
    mirror = jnp.where(first_offset, spread(own[:, :, 24:], 1, 1), spread(own[:, :, 24:], 2, 0))
    parts = jnp.concatenate([spread(own[:, :, :24], 0, 2), mirror], axis=2)
    send = lambda picks, by: from_behind(jnp.stack([parts[d] for d in picks]).astype(bf16), "ka", by).astype(f32)
    plus_one = send((1, 5, 9), 1)
    plus_two = send((2, 6), 2)
    minus_one = send((3, 7), -1)
    low = parts[0] + plus_one[0] + plus_two[0]
    high = parts[8] + plus_one[2] + minus_one[1]
    total = parts[4] + plus_one[1] + plus_two[1] + minus_one[0]
    total = total + from_behind(low, "ka", -4) + from_behind(high, "ka", 4)
    return arrange(ga_word, total)


def solution(mesh):
    in_specs = (
        P("ka", None, None, None),
        P(None, None, "ga"),
        P(None, None, ("ga", "ka"), None),
        P("ka", None, None),
    )
    out_specs = P("ka", None, None, "ga")
    return jax.shard_map(body, mesh=mesh, in_specs=in_specs, out_specs=out_specs, check_vma=False)
```

```python
import functools
import jax
import jax.numpy as jnp
from jax import lax
from jax.experimental import pallas as pl
from jax.experimental.pallas import tpu as pltpu
from jax.sharding import PartitionSpec as P

f32 = jnp.float32
bf16 = jnp.bfloat16

WIN = 8
KB = 6
PAIRS = 72
TOTAL = WIN * PAIRS
CHUNK = 16
SLOTS = 22
CHUNKS = (TOTAL + SLOTS * (CHUNK - 1)) // CHUNK // 2 * 2 + 2
MSG = 112
VMEM_LIMIT = 36 * 2**20


def from_behind(x, axis, by):
    count = lax.axis_size(axis)
    return lax.ppermute(x, axis, [(i, (i + by) % count) for i in range(count)])


def half_swap(mask, first, second):
    return jnp.where(mask, first, pltpu.roll(second, 4, 0))


def density_kernel(count, ends, steps, *refs):
    pair_refs = refs[:count]
    zv_ref, zc_ref = refs[count : count + 2]
    mv_ref, mc_ref, left, right, va, ca, vb, cb = refs[-8:]
    step = pl.program_id(0)
    low = lax.broadcasted_iota(jnp.int32, (8, 1024), 0) < 4

    def produce(chunk, v_buf, c_buf):
        block = chunk // 3
        jh = chunk % 3
        if ends:
            block = block + jnp.where(block >= 2, 4, 0)
        for cv, buf in ((0, v_buf), (1, c_buf)):
            for jl in range(2):
                point = block * KB + 2 * jh + jl
                for part in range(4):
                    cols = slice(256 * part, 256 * part + 256)
                    imag_cols = slice(1024 + 256 * part, 1280 + 256 * part)
                    lefts = []
                    for band in range(4):
                        row = 4 * cv + band
                        lr = jnp.broadcast_to(left[point, row : row + 1, cols], (8, 256))
                        li = jnp.broadcast_to(left[point, 8 + row : 9 + row, cols], (8, 256))
                        lefts.append((lr, li))
                    for o in range(2):
                        for p in range(3):
                            rr = right[(block + o) * 3 + p, cv, 0, :, cols]
                            ri = right[(block + o) * 3 + p, cv, 1, :, cols]
                            base = ((jl * 2 + o) * 3 + p) * 32
                            for half in range(2):
                                reals = []
                                imags = []
                                for lr, li in lefts[2 * half : 2 * half + 2]:
                                    reals.append(lr * rr + li * ri)
                                    imags.append(lr * ri - li * rr)
                                rows = slice(base + 16 * half, base + 16 * half + 16)
                                buf[rows, cols] = jnp.concatenate(reals, axis=0).astype(bf16)
                                buf[rows, imag_cols] = jnp.concatenate(imags, axis=0).astype(bf16)
                    yield

    def consume(sub, v_buf, c_buf):
        mask = lax.broadcasted_iota(jnp.int32, (8, 256), 0) < 4
        for buf, z_ref, out_ref in ((v_buf, zv_ref, mv_ref), (c_buf, zc_ref, mc_ref)):
            for tile in range(z_ref.shape[1] // 256):
                cols = slice(256 * tile, 256 * tile + 256)
                for jl in range(2):
                    res = jnp.dot(buf[192 * jl : 192 * jl + 192], z_ref[:, cols], preferred_element_type=f32)
                    for o in range(2):
                        for p in range(3):
                            base = (o * 3 + p) * 32
                            a = [res[base + 8 * c : base + 8 * c + 8] for c in range(4)]
                            first = [half_swap(mask, a[0], a[1]), half_swap(mask, a[2], a[3])]
                            second = [
                                jnp.where(mask, pltpu.roll(a[0], 4, 0), a[1]),
                                jnp.where(mask, pltpu.roll(a[2], 4, 0), a[3]),
                            ]
                            for jj, value in ((0, first), (1, second)):
                                index = sub * 24 + (2 * p + jj) * 4 + jl * 2 + o
                                out_ref[index, :, cols] = jnp.concatenate(value, axis=0).astype(bf16)
                    yield

    def drain(*generators):
        live = list(generators)
        while live:
            live = [g for g in live if next(g, True) is None]

    @pl.when(step == 0)
    def _():
        for b in range(2 * count):
            for j in range(KB):
                x = pair_refs[b // 2][b % 2, 16 * j : 16 * j + 16, :].astype(f32)
                left[b * KB + j] = x
                if b > 0:
                    index = (b - 1) * 3 + j // 2
                    for r in range(2):
                        half = x[8 * r : 8 * r + 8]
                        turned = pltpu.roll(half, 4, 0)
                        if j % 2 == 0:
                            right[index, 0, r] = half
                            right[index, 1, r] = turned
                        else:
                            right[index, 0, r] = jnp.where(low, right[index, 0, r], turned)
                            right[index, 1, r] = jnp.where(low, right[index, 1, r], half)
        drain(produce(0, va, ca))

    drain(consume(0, va, ca), produce(2 * step + 1, vb, cb))
    drain(consume(1, vb, cb), produce(jnp.minimum(2 * step + 2, 2 * steps - 1), va, ca))


def densities(pairs, ends, zv, zc, previous):
    whole = lambda shape: pl.BlockSpec(shape, lambda n: (0,) * len(shape), pipeline_mode=pl.Buffered(1))
    operands = list(pairs) + [zv, zc]
    in_specs = [whole(x.shape) for x in operands]
    aliases = {}
    if previous is not None:
        aliases = {len(operands): 0, len(operands) + 1: 1}
        in_specs += [pl.BlockSpec(memory_space=pl.ANY)] * 2
        operands += list(previous)
    count = len(pairs)
    steps = 6
    place = (lambda n: (n + jnp.where(n >= 3, 6, 0), 0, 0)) if ends else (lambda n: (3 + n, 0, 0))
    wv = zv.shape[1]
    wc = zc.shape[1]
    return pl.pallas_call(
        functools.partial(density_kernel, count, ends, steps),
        grid=(steps,),
        in_specs=in_specs,
        out_specs=[pl.BlockSpec((48, 16, wv), place), pl.BlockSpec((48, 16, wc), place)],
        out_shape=[
            jax.ShapeDtypeStruct((TOTAL, 16, wv), bf16),
            jax.ShapeDtypeStruct((TOTAL, 16, wc), bf16),
        ],
        scratch_shapes=[
            pltpu.VMEM((2 * count * KB, 16, 1024), f32),
            pltpu.VMEM(((2 * count - 1) * 3, 2, 2, 8, 1024), f32),
            pltpu.VMEM((384, 2048), bf16),
            pltpu.VMEM((384, 2048), bf16),
            pltpu.VMEM((384, 2048), bf16),
            pltpu.VMEM((384, 2048), bf16),
        ],
        input_output_aliases=aliases,
        compiler_params=pltpu.CompilerParams(vmem_limit_bytes=28 * 2**20),
        cost_estimate=pl.CostEstimate(
            flops=2 * steps * 48 * 16 * 2048 * (wv + wc), bytes_accessed=steps * 3 * 2**20, transcendentals=0
        ),
        name="densities",
    )(*operands)


def quarter_rows():
    own = [[(0, 0, 0, 16)], [(0, 16, 0, 8), (1, 0, 8, 8)], [(1, 8, 0, 16)]]
    own += [[(q + 2, r, s, n) for q, r, s, n in item] for item in own]
    mirror = [[(0, 24)], [(0, 40), (1, 24)], [(1, 40)]]
    mirror += [[(q + 2, r) for q, r in item] for item in mirror]
    return own, mirror


def apply_kernel(order_ref, slot_ref, used_ref, ga_ref, mv_ref, mc_ref, w_ref, out_ref, rhs, xv):
    ga = ga_ref[0]
    lane_group = lax.broadcasted_iota(jnp.int32, (16, 128), 1) >> 5
    spots = [(((q & 1) ^ (ga & 1)) << 1) | ((q >> 1) ^ (ga >> 1)) for q in range(4)]
    own_rows, mirror_rows = quarter_rows()

    def build(slot, carry):
        for x in range(4):
            wr = w_ref[x, slot, 0]
            wi = w_ref[x, slot, 1]
            rhs[slot, 64 * x : 64 * x + 64, 0:128] = wr
            rhs[slot, 64 * x : 64 * x + 64, 128:256] = -wi
            rhs[slot, 256 + 64 * x : 320 + 64 * x, 0:128] = wi
            rhs[slot, 256 + 64 * x : 320 + 64 * x, 128:256] = wr
        return carry

    lax.fori_loop(0, SLOTS, build, 0)

    def chunk(q, carry):
        for u in range(2):
            slot = slot_ref[2 * q + u]
            ids = [order_ref[(2 * q + u) * CHUNK + i] for i in range(CHUNK)]
            sources = [jnp.minimum(i, TOTAL - 1) for i in ids]
            lhs = jnp.concatenate([mv_ref[s] for s in sources], axis=0)
            res = jnp.dot(lhs, rhs[slot], preferred_element_type=f32).astype(bf16)
            for i in range(CHUNK):
                xv[ids[i]] = res[16 * i : 16 * i + 16]
        return carry

    lax.fori_loop(0, (used_ref[0] + 1) >> 1, chunk, 0)

    def contract(t, carry):
        for jh in range(3):
            for h in range(3):
                first = ((t * 3 + jh) * 6 + 2 * h) * 4
                rows = []
                for i in range(8):
                    y = mc_ref[first + i]
                    rows.append(y)
                    rows.append(jnp.concatenate([-y[:, 128:], y[:, :128]], axis=1))
                lhs = jnp.concatenate([xv[first + i] for i in range(8)], axis=0)
                d = lax.dot_general(
                    lhs, jnp.concatenate(rows, axis=0), (((1,), (1,)), ((), ())), preferred_element_type=f32
                )
                blocks = [
                    [d[16 * i : 16 * i + 16, 128 * (i // 4) : 128 * (i // 4) + 128] for i in range(4 * l, 4 * l + 4)]
                    for l in range(2)
                ]
                odd = (lane_group & 1) == 1
                low = lane_group < 2
                mixed = [[jnp.where(odd, b[2 * jl + 1], b[2 * jl]) for jl in range(2)] for b in blocks]
                for l in range(2):
                    own = jnp.where(low, mixed[l][0], mixed[l][1])
                    for q, r, s, n in own_rows[2 * h + l]:
                        out_ref[spots[q], t, jh, r : r + n, :] = own[s : s + n]
                for jl in range(2):
                    if jl == 0:
                        mirror = jnp.where(low, mixed[0][0], pltpu.roll(mixed[1][0], 64, 1))
                    else:
                        mirror = jnp.where(low, pltpu.roll(mixed[0][1], 64, 1), mixed[1][1])
                    for q, r in mirror_rows[2 * jh + jl]:
                        out_ref[spots[q], t, h, r : r + 16, :] = mirror
        return carry

    lax.fori_loop(0, WIN, contract, 0)


def apply_screened(order, slots, used, ga, mv, mc, w):
    smem = pl.BlockSpec(memory_space=pltpu.SMEM)
    vmem = pl.BlockSpec(memory_space=pltpu.VMEM)
    return pl.pallas_call(
        apply_kernel,
        in_specs=[smem] * 4 + [vmem] * 3,
        out_specs=vmem,
        out_shape=jax.ShapeDtypeStruct((4, WIN, 3, 56, 128), f32),
        scratch_shapes=[
            pltpu.VMEM((SLOTS, 512, 256), bf16),
            pltpu.VMEM((TOTAL + 1, 16, 256), bf16),
        ],
        compiler_params=pltpu.CompilerParams(vmem_limit_bytes=VMEM_LIMIT),
        cost_estimate=pl.CostEstimate(flops=6 * 10**9, bytes_accessed=18 * 2**20, transcendentals=0),
        name="apply_screened",
    )(order, slots, used, ga, mv, mc, w)


def split_dot(x, sel):
    high = x.astype(bf16)
    low = (x - high.astype(f32)).astype(bf16)
    return jnp.dot(high, sel, preferred_element_type=f32) + jnp.dot(low, sel, preferred_element_type=f32)


def arrange_kernel(ga_ref, parts_ref, out_ref):
    ga = ga_ref[0]
    src = lax.broadcasted_iota(jnp.int32, (128, 384), 0)
    lane = lax.broadcasted_iota(jnp.int32, (128, 384), 1)
    row = lax.broadcasted_iota(jnp.int32, (32, 384), 0)
    row_lane = lax.broadcasted_iota(jnp.int32, (32, 384), 1)
    start = ga + (ga >> 1)
    outer = row_lane >> 6
    place = 6 * ga + outer
    own = (24, (lane >> 4) & 3, lane & 3, outer * 4 + ((row_lane >> 2) & 3))
    mirror = (32, lane & 3, (lane >> 4) & 3, ((place >> 2) - start) * 16 + ((row_lane >> 2) & 3) * 4 + (place & 3))
    for kind, (count, c, c2, wanted) in enumerate((own, mirror)):
        low = 24 * kind
        x = jnp.concatenate([parts_ref[jh, low : low + count, :] for jh in range(3)], axis=0)
        keep = row[:count] == wanted[:count]
        for combo in range(8):
            sel = (src == combo * 16 + c * 4 + c2).astype(f32).astype(bf16)
            spread = split_dot(x, sel)
            for jh in range(3):
                rows = spread[count * jh : count * jh + count]
                picked = jnp.sum(jnp.where(keep, rows, 0.0), axis=0, keepdims=True)
                if kind == 1 and combo % 2 == 1:
                    picked = -picked
                out_ref[2 * jh + combo // 4, 2 * kind + (combo // 2) % 2, pl.ds(combo % 2, 1), :] = picked


def arrange(ga, parts):
    vmem = pl.BlockSpec(memory_space=pltpu.VMEM)
    return pl.pallas_call(
        arrange_kernel,
        in_specs=[pl.BlockSpec(memory_space=pltpu.SMEM), vmem],
        out_specs=vmem,
        out_shape=jax.ShapeDtypeStruct((KB, 4, 2, 384), f32),
        compiler_params=pltpu.CompilerParams(vmem_limit_bytes=VMEM_LIMIT),
        name="arrange",
    )(ga, parts)


def schedule(slots):
    pair = jnp.arange(TOTAL, dtype=jnp.int32)
    names = jnp.arange(SLOTS, dtype=jnp.int32)
    hot = slots[:, None] == names[None, :]
    needed = (jnp.sum(hot.astype(jnp.int32), axis=0) + CHUNK - 1) // CHUNK
    start = jnp.sum(jnp.where(names[:, None] < names[None, :], needed[:, None], 0), axis=0)
    same = (slots[:, None] == slots[None, :]) & (pair[None, :] < pair[:, None])
    rank = jnp.sum(same.astype(jnp.int32), axis=1)
    place = jnp.sum(jnp.where(hot, start[None, :], 0), axis=1) * CHUNK + rank
    seat = jnp.arange(CHUNKS * CHUNK, dtype=jnp.int32)
    taken = place[None, :] == seat[:, None]
    order = TOTAL + jnp.sum(jnp.where(taken, pair[None, :] - TOTAL, 0), axis=1)
    chunk = jnp.arange(CHUNKS, dtype=jnp.int32)
    ended = (start + needed)[None, :] <= chunk[:, None]
    slot_of = jnp.minimum(jnp.sum(ended.astype(jnp.int32), axis=1), SLOTS - 1)
    return order, slot_of, jnp.sum(needed).reshape(1)


def zeta_matrix(zeta):
    zr = zeta[:, 0]
    zi = zeta[:, 1]
    return jnp.concatenate([jnp.concatenate([zr, zi], axis=1), jnp.concatenate([-zi, zr], axis=1)], axis=0)


def body(bloch_samples, zeta_vectors, screened, pair_slots):
    ka_count = lax.axis_size("ka")
    ka = lax.axis_index("ka")
    ga = lax.axis_index("ga")
    ga_word = ga.reshape(1).astype(jnp.int32)
    part = lax.rem(ka, WIN)
    slots = jnp.transpose(pair_slots.reshape(3, 2, 2, KB), (0, 3, 1, 2)).reshape(1, PAIRS)
    tail = jnp.pad(slots.astype(bf16), ((0, 15), (0, 1024 - PAIRS)))
    message = jnp.concatenate([bloch_samples.reshape(96, 1024), tail], axis=0)
    following = from_behind(message, "ka", -1)
    zv = zeta_matrix(zeta_vectors)
    mine = lax.dynamic_slice_in_dim(zeta_vectors, 128 * lax.rem(part, 2), 128, 2)
    mine, following = lax.optimization_barrier((mine, following))
    holders = [(k, (k % WIN) // 2) for k in range(ka_count)]
    over = lax.ppermute(mine, ("ka", "ga"), [(4 * k + h, 4 * k + (h ^ 2)) for k, h in holders])
    pieces = jnp.transpose(screened.reshape(SLOTS, 2, 4, WIN, 128), (3, 0, 1, 2, 4))
    pieces = jnp.concatenate([pieces, pieces], axis=0)
    pieces, following = lax.optimization_barrier((pieces, following))
    line = 2 * WIN
    near_groups = [[x * line + s for s in range(line)] for x in range(ka_count // line)]
    x_groups = [[x * line + s for x in range(ka_count // line)] for s in range(line)]
    pieces = lax.all_to_all(pieces, "ka", 0, 0, axis_index_groups=near_groups, tiled=True)
    rows = jnp.transpose(pieces, (1, 2, 0, 3, 4)).reshape(SLOTS, 2, 4 * line, 128)
    held = jnp.where(ga == part // 2, mine, over)
    moves = [(4 * k + h, 4 * k + (h ^ 1)) for k, h in holders]
    moves += [(4 * k + (h ^ 2), 4 * k + (h ^ 3)) for k, h in holders]
    zc = zeta_matrix(held + lax.ppermute(held, ("ka", "ga"), moves))
    here = jnp.stack([message, following])
    ahead = from_behind(here, "ka", -2)
    behind = from_behind(here, "ka", 2)
    rows, ahead, behind, zv = lax.optimization_barrier((rows, ahead, behind, zv))
    w = lax.all_gather(rows, "ka", axis_index_groups=x_groups)
    ahead2 = from_behind(ahead, "ka", -2)
    behind2 = from_behind(behind, "ka", 2)
    made = densities((behind, here, ahead), False, zv, zc, None)
    made = densities((behind2, behind, here, ahead, ahead2), True, zv, zc, made)
    mv, mc, *pairs = lax.optimization_barrier((*made, behind2, behind, here, ahead))
    all_slots = jnp.concatenate([x[:, 96, :PAIRS] for x in pairs], axis=0).reshape(TOTAL)
    order, slot_of, used = schedule(all_slots.astype(jnp.int32))
    partial = apply_screened(order, slot_of, used, ga_word, mv, mc, w)
    arrived = lax.ppermute(partial[2:].astype(bf16), "ga", [(0, 1), (1, 0), (2, 3), (3, 2)])
    own = partial[0] + arrived[0].astype(f32)
    other = (partial[1] + arrived[1].astype(f32)).astype(bf16)
    own = own + lax.ppermute(other, "ga", [(0, 2), (2, 0), (1, 3), (3, 1)]).astype(f32)
    first_offset = ((lax.broadcasted_iota(jnp.int32, (1, 1, 1, 128), 3) >> 5) & 1) == 0
    spread = lambda x, before, after: jnp.pad(x, ((before, after), (0, 0), (0, 0), (0, 0)))
    mirror = jnp.where(first_offset, spread(own[:, :, 24:], 1, 1), spread(own[:, :, 24:], 2, 0))
    parts = jnp.concatenate([spread(own[:, :, :24], 0, 2), mirror], axis=2)
    send = lambda picks, by: from_behind(jnp.stack([parts[d] for d in picks]).astype(bf16), "ka", by).astype(f32)
    plus_one = send((1, 5, 9), 1)
    plus_two = send((2, 6), 2)
    minus_one = send((3, 7), -1)
    low = parts[0] + plus_one[0] + plus_two[0]
    high = parts[8] + plus_one[2] + minus_one[1]
    total = parts[4] + plus_one[1] + plus_two[1] + minus_one[0]
    total = total + from_behind(low, "ka", -4) + from_behind(high, "ka", 4)
    return arrange(ga_word, total)


def solution(mesh):
    in_specs = (
        P("ka", None, None, None),
        P(None, None, "ga"),
        P(None, None, ("ga", "ka"), None),
        P("ka", None, None),
    )
    out_specs = P("ka", None, None, "ga")
    return jax.shard_map(body, mesh=mesh, in_specs=in_specs, out_specs=out_specs, check_vma=False)
```

```python
import functools
import jax
import jax.numpy as jnp
from jax import lax
from jax.experimental import pallas as pl
from jax.experimental.pallas import tpu as pltpu
from jax.sharding import PartitionSpec as P

f32 = jnp.float32
bf16 = jnp.bfloat16

WIN = 8
KB = 6
PAIRS = 72
TOTAL = WIN * PAIRS
CHUNK = 16
SLOTS = 22
UNROLL = 4
CHUNKS = (TOTAL + SLOTS * (CHUNK - 1)) // CHUNK // UNROLL * UNROLL + UNROLL
MSG = 112
VMEM_LIMIT = 50 * 2**20


def from_behind(x, axis, by):
    count = lax.axis_size(axis)
    return lax.ppermute(x, axis, [(i, (i + by) % count) for i in range(count)])


def half_swap(mask, first, second):
    return jnp.where(mask, first, pltpu.roll(second, 4, 0))


def density_kernel(count, rest, steps, *refs):
    pair_refs = refs[:count]
    zv_ref, zc_ref = refs[count : count + 2]
    mv_ref, mc_ref, slots_ref, left, right, va, ca, vb, cb = refs[-9:]
    step = pl.program_id(0)
    low = lax.broadcasted_iota(jnp.int32, (8, 1024), 0) < 4

    def produce(chunk, v_buf, c_buf):
        block = chunk // 3
        jh = chunk % 3
        if rest:
            block = block + jnp.where(block >= 4, 2, 0)
        for cv, buf in ((0, v_buf), (1, c_buf)):
            for jl in range(2):
                point = block * KB + 2 * jh + jl
                for part in range(4):
                    cols = slice(256 * part, 256 * part + 256)
                    imag_cols = slice(1024 + 256 * part, 1280 + 256 * part)
                    lefts = []
                    for band in range(4):
                        row = 4 * cv + band
                        lr = jnp.broadcast_to(left[point, row : row + 1, cols], (8, 256))
                        li = jnp.broadcast_to(left[point, 8 + row : 9 + row, cols], (8, 256))
                        lefts.append((lr, li))
                    for o in range(2):
                        for p in range(3):
                            rr = right[(block + o) * 3 + p, cv, 0, :, cols]
                            ri = right[(block + o) * 3 + p, cv, 1, :, cols]
                            base = ((jl * 2 + o) * 3 + p) * 32
                            for half in range(2):
                                reals = []
                                imags = []
                                for lr, li in lefts[2 * half : 2 * half + 2]:
                                    reals.append(lr * rr + li * ri)
                                    imags.append(lr * ri - li * rr)
                                rows = slice(base + 16 * half, base + 16 * half + 16)
                                buf[rows, cols] = jnp.concatenate(reals, axis=0).astype(bf16)
                                buf[rows, imag_cols] = jnp.concatenate(imags, axis=0).astype(bf16)
                    yield

    def consume(sub, v_buf, c_buf):
        mask = lax.broadcasted_iota(jnp.int32, (8, 256), 0) < 4
        for buf, z_ref, out_ref in ((v_buf, zv_ref, mv_ref), (c_buf, zc_ref, mc_ref)):
            for tile in range(z_ref.shape[1] // 256):
                cols = slice(256 * tile, 256 * tile + 256)
                for jl in range(2):
                    res = jnp.dot(buf[192 * jl : 192 * jl + 192], z_ref[:, cols], preferred_element_type=f32)
                    for o in range(2):
                        for p in range(3):
                            base = (o * 3 + p) * 32
                            a = [res[base + 8 * c : base + 8 * c + 8] for c in range(4)]
                            first = [half_swap(mask, a[0], a[1]), half_swap(mask, a[2], a[3])]
                            second = [
                                jnp.where(mask, pltpu.roll(a[0], 4, 0), a[1]),
                                jnp.where(mask, pltpu.roll(a[2], 4, 0), a[3]),
                            ]
                            for jj, value in ((0, first), (1, second)):
                                index = sub * 24 + (2 * p + jj) * 4 + jl * 2 + o
                                out_ref[index, :, cols] = jnp.concatenate(value, axis=0).astype(bf16)
                    yield

    def drain(*generators):
        live = list(generators)
        while live:
            live = [g for g in live if next(g, True) is None]

    @pl.when(step == 0)
    def _():
        for b in range(2 * count):
            if b < WIN:
                tail = pair_refs[b // 2][b % 2, 96:112, 0:128].astype(f32)
                slots_ref[b : b + 1, :] = tail[0:1].astype(jnp.int32)
            for j in range(KB):
                x = pair_refs[b // 2][b % 2, 16 * j : 16 * j + 16, :].astype(f32)
                left[b * KB + j] = x
                if b > 0:
                    index = (b - 1) * 3 + j // 2
                    for r in range(2):
                        half = x[8 * r : 8 * r + 8]
                        turned = pltpu.roll(half, 4, 0)
                        if j % 2 == 0:
                            right[index, 0, r] = half
                            right[index, 1, r] = turned
                        else:
                            right[index, 0, r] = jnp.where(low, right[index, 0, r], turned)
                            right[index, 1, r] = jnp.where(low, right[index, 1, r], half)
        drain(produce(0, va, ca))

    drain(consume(0, va, ca), produce(2 * step + 1, vb, cb))
    drain(consume(1, vb, cb), produce(jnp.minimum(2 * step + 2, 2 * steps - 1), va, ca))


def densities(pairs, rest, zv, zc, previous):
    whole = lambda shape: pl.BlockSpec(shape, lambda n: (0,) * len(shape), pipeline_mode=pl.Buffered(1))
    operands = list(pairs) + [zv, zc]
    in_specs = [whole(x.shape) for x in operands]
    aliases = {}
    if previous is not None:
        aliases = {len(operands): 0, len(operands) + 1: 1}
        in_specs += [pl.BlockSpec(memory_space=pl.ANY)] * 2
        operands += list(previous)
    count = len(pairs)
    steps = 9 if rest else 3
    place = (lambda n: (n + jnp.where(n >= 6, 3, 0), 0, 0)) if rest else (lambda n: (6 + n, 0, 0))
    wv = zv.shape[1]
    wc = zc.shape[1]
    return pl.pallas_call(
        functools.partial(density_kernel, count, rest, steps),
        grid=(steps,),
        in_specs=in_specs,
        out_specs=[
            pl.BlockSpec((48, 16, wv), place),
            pl.BlockSpec((48, 16, wc), place),
            pl.BlockSpec((min(2 * count, WIN), 128), lambda n: (0, 0)),
        ],
        out_shape=[
            jax.ShapeDtypeStruct((TOTAL, 16, wv), bf16),
            jax.ShapeDtypeStruct((TOTAL, 16, wc), bf16),
            jax.ShapeDtypeStruct((min(2 * count, WIN), 128), jnp.int32),
        ],
        scratch_shapes=[
            pltpu.VMEM((2 * count * KB, 16, 1024), f32),
            pltpu.VMEM(((2 * count - 1) * 3, 2, 2, 8, 1024), f32),
            pltpu.VMEM((384, 2048), bf16),
            pltpu.VMEM((384, 2048), bf16),
            pltpu.VMEM((384, 2048), bf16),
            pltpu.VMEM((384, 2048), bf16),
        ],
        input_output_aliases=aliases,
        compiler_params=pltpu.CompilerParams(vmem_limit_bytes=VMEM_LIMIT),
        cost_estimate=pl.CostEstimate(
            flops=2 * steps * 48 * 16 * 2048 * (wv + wc), bytes_accessed=steps * 3 * 2**20, transcendentals=0
        ),
        name="densities",
    )(*operands)


def quarter_rows():
    own = [[(0, 0, 0, 16)], [(0, 16, 0, 8), (1, 0, 8, 8)], [(1, 8, 0, 16)]]
    own += [[(q + 2, r, s, n) for q, r, s, n in item] for item in own]
    mirror = [[(0, 24)], [(0, 40), (1, 24)], [(1, 40)]]
    mirror += [[(q + 2, r) for q, r in item] for item in mirror]
    return own, mirror


def apply_kernel(order_ref, slot_ref, used_ref, ga_ref, mv_hbm, mc_hbm, w_ref, out_ref, rhs, xv, mv_ref, mc_ref, done):
    fetch_v = pltpu.make_async_copy(mv_hbm, mv_ref, done.at[0])
    fetch_c = pltpu.make_async_copy(mc_hbm, mc_ref, done.at[1])
    fetch_v.start()
    fetch_c.start()
    ga = ga_ref[0]
    lane_group = lax.broadcasted_iota(jnp.int32, (16, 128), 1) >> 5
    spots = [(((q & 1) ^ (ga & 1)) << 1) | ((q >> 1) ^ (ga >> 1)) for q in range(4)]
    own_rows, mirror_rows = quarter_rows()

    def build(slot, carry):
        for x in range(4):
            wr = w_ref[x, slot, 0]
            wi = w_ref[x, slot, 1]
            rhs[slot, 64 * x : 64 * x + 64, 0:128] = wr
            rhs[slot, 64 * x : 64 * x + 64, 128:256] = -wi
            rhs[slot, 256 + 64 * x : 320 + 64 * x, 0:128] = wi
            rhs[slot, 256 + 64 * x : 320 + 64 * x, 128:256] = wr
        return carry

    lax.fori_loop(0, SLOTS, build, 0)
    fetch_v.wait()

    def chunk(q, carry):
        for u in range(UNROLL):
            slot = slot_ref[UNROLL * q + u]
            ids = [order_ref[(UNROLL * q + u) * CHUNK + i] for i in range(CHUNK)]
            sources = [jnp.minimum(i, TOTAL - 1) for i in ids]
            lhs = jnp.concatenate([mv_ref[s] for s in sources], axis=0)
            res = jnp.dot(lhs, rhs[slot], preferred_element_type=f32).astype(bf16)
            for i in range(CHUNK):
                xv[ids[i]] = res[16 * i : 16 * i + 16]
        return carry

    lax.fori_loop(0, (used_ref[0] + UNROLL - 1) >> 2, chunk, 0)
    fetch_c.wait()

    def contract(t, carry):
        for jh in range(3):
            for h in range(3):
                first = ((t * 3 + jh) * 6 + 2 * h) * 4
                rows = []
                for i in range(8):
                    y = mc_ref[first + i]
                    rows.append(y)
                    rows.append(jnp.concatenate([-y[:, 128:], y[:, :128]], axis=1))
                lhs = jnp.concatenate([xv[first + i] for i in range(8)], axis=0)
                d = lax.dot_general(
                    lhs, jnp.concatenate(rows, axis=0), (((1,), (1,)), ((), ())), preferred_element_type=f32
                )
                blocks = [
                    [d[16 * i : 16 * i + 16, 128 * (i // 4) : 128 * (i // 4) + 128] for i in range(4 * l, 4 * l + 4)]
                    for l in range(2)
                ]
                odd = (lane_group & 1) == 1
                low = lane_group < 2
                mixed = [[jnp.where(odd, b[2 * jl + 1], b[2 * jl]) for jl in range(2)] for b in blocks]
                for l in range(2):
                    own = jnp.where(low, mixed[l][0], mixed[l][1])
                    for q, r, s, n in own_rows[2 * h + l]:
                        out_ref[spots[q], t, jh, r : r + n, :] = own[s : s + n]
                for jl in range(2):
                    if jl == 0:
                        mirror = jnp.where(low, mixed[0][0], pltpu.roll(mixed[1][0], 64, 1))
                    else:
                        mirror = jnp.where(low, pltpu.roll(mixed[0][1], 64, 1), mixed[1][1])
                    for q, r in mirror_rows[2 * jh + jl]:
                        out_ref[spots[q], t, h, r : r + 16, :] = mirror
        return carry

    lax.fori_loop(0, WIN, contract, 0)


def apply_screened(order, slots, used, ga, mv, mc, w):
    smem = pl.BlockSpec(memory_space=pltpu.SMEM)
    vmem = pl.BlockSpec(memory_space=pltpu.VMEM)
    return pl.pallas_call(
        apply_kernel,
        in_specs=[smem] * 4 + [pl.BlockSpec(memory_space=pl.ANY)] * 2 + [vmem],
        out_specs=vmem,
        out_shape=jax.ShapeDtypeStruct((4, WIN, 3, 56, 128), f32),
        scratch_shapes=[
            pltpu.VMEM((SLOTS, 512, 256), bf16),
            pltpu.VMEM((TOTAL + 1, 16, 256), bf16),
            pltpu.VMEM(mv.shape, bf16),
            pltpu.VMEM(mc.shape, bf16),
            pltpu.SemaphoreType.DMA((2,)),
        ],
        compiler_params=pltpu.CompilerParams(vmem_limit_bytes=VMEM_LIMIT),
        cost_estimate=pl.CostEstimate(flops=6 * 10**9, bytes_accessed=18 * 2**20, transcendentals=0),
        name="apply_screened",
    )(order, slots, used, ga, mv, mc, w)


def split_dot(x, sel):
    high = x.astype(bf16)
    low = (x - high.astype(f32)).astype(bf16)
    return jnp.dot(high, sel, preferred_element_type=f32) + jnp.dot(low, sel, preferred_element_type=f32)


def arrange_kernel(ga_ref, parts_ref, out_ref):
    ga = ga_ref[0]
    src = lax.broadcasted_iota(jnp.int32, (128, 384), 0)
    lane = lax.broadcasted_iota(jnp.int32, (128, 384), 1)
    row = lax.broadcasted_iota(jnp.int32, (32, 384), 0)
    row_lane = lax.broadcasted_iota(jnp.int32, (32, 384), 1)
    start = ga + (ga >> 1)
    outer = row_lane >> 6
    place = 6 * ga + outer
    own = (24, (lane >> 4) & 3, lane & 3, outer * 4 + ((row_lane >> 2) & 3))
    mirror = (32, lane & 3, (lane >> 4) & 3, ((place >> 2) - start) * 16 + ((row_lane >> 2) & 3) * 4 + (place & 3))
    for kind, (count, c, c2, wanted) in enumerate((own, mirror)):
        low = 24 * kind
        x = jnp.concatenate([parts_ref[jh, low : low + count, :] for jh in range(3)], axis=0)
        keep = row[:count] == wanted[:count]
        for combo in range(8):
            sel = (src == combo * 16 + c * 4 + c2).astype(f32).astype(bf16)
            spread = split_dot(x, sel)
            for jh in range(3):
                rows = spread[count * jh : count * jh + count]
                picked = jnp.sum(jnp.where(keep, rows, 0.0), axis=0, keepdims=True)
                if kind == 1 and combo % 2 == 1:
                    picked = -picked
                out_ref[2 * jh + combo // 4, 2 * kind + (combo // 2) % 2, pl.ds(combo % 2, 1), :] = picked


def arrange(ga, parts):
    vmem = pl.BlockSpec(memory_space=pltpu.VMEM)
    return pl.pallas_call(
        arrange_kernel,
        in_specs=[pl.BlockSpec(memory_space=pltpu.SMEM), vmem],
        out_specs=vmem,
        out_shape=jax.ShapeDtypeStruct((KB, 4, 2, 384), f32),
        compiler_params=pltpu.CompilerParams(vmem_limit_bytes=VMEM_LIMIT),
        name="arrange",
    )(ga, parts)


def schedule(slots):
    pair = jnp.arange(TOTAL, dtype=jnp.int32)
    names = jnp.arange(SLOTS, dtype=jnp.int32)
    hot = slots[:, None] == names[None, :]
    needed = (jnp.sum(hot.astype(jnp.int32), axis=0) + CHUNK - 1) // CHUNK
    start = jnp.sum(jnp.where(names[:, None] < names[None, :], needed[:, None], 0), axis=0)
    same = (slots[:, None] == slots[None, :]) & (pair[None, :] < pair[:, None])
    rank = jnp.sum(same.astype(jnp.int32), axis=1)
    place = jnp.sum(jnp.where(hot, start[None, :], 0), axis=1) * CHUNK + rank
    seat = jnp.arange(CHUNKS * CHUNK, dtype=jnp.int32)
    taken = place[None, :] == seat[:, None]
    order = TOTAL + jnp.sum(jnp.where(taken, pair[None, :] - TOTAL, 0), axis=1)
    chunk = jnp.arange(CHUNKS, dtype=jnp.int32)
    ended = (start + needed)[None, :] <= chunk[:, None]
    slot_of = jnp.minimum(jnp.sum(ended.astype(jnp.int32), axis=1), SLOTS - 1)
    return order, slot_of, jnp.sum(needed).reshape(1)


def zeta_matrix(zeta):
    zr = zeta[:, 0]
    zi = zeta[:, 1]
    return jnp.concatenate([jnp.concatenate([zr, zi], axis=1), jnp.concatenate([-zi, zr], axis=1)], axis=0)


def body(bloch_samples, zeta_vectors, screened, pair_slots):
    ka_count = lax.axis_size("ka")
    ka = lax.axis_index("ka")
    ga = lax.axis_index("ga")
    ga_word = ga.reshape(1).astype(jnp.int32)
    part = lax.rem(ka, WIN)
    slots = jnp.transpose(pair_slots.reshape(3, 2, 2, KB), (0, 3, 1, 2)).reshape(1, PAIRS)
    tail = jnp.pad(slots.astype(bf16), ((0, 15), (0, 1024 - PAIRS)))
    message = jnp.concatenate([bloch_samples.reshape(96, 1024), tail], axis=0)
    following = from_behind(message, "ka", -1)
    here = jnp.stack([message, following])
    ahead = from_behind(here, "ka", -2)
    behind = from_behind(here, "ka", 2)
    zv = zeta_matrix(zeta_vectors)
    mine = lax.dynamic_slice_in_dim(zeta_vectors, 128 * lax.rem(part, 2), 128, 2)
    halves = lax.all_gather(mine, "ga")
    zc = zeta_matrix(lax.dynamic_index_in_dim(halves, part // 2, 0, keepdims=False))
    pieces = jnp.transpose(screened.reshape(SLOTS, 2, 4, WIN, 128), (3, 0, 1, 2, 4))
    pieces = jnp.concatenate([pieces, pieces], axis=0)
    pieces = pieces + following[0, 0] * 0
    line = 2 * WIN
    near_groups = [[x * line + s for s in range(line)] for x in range(ka_count // line)]
    x_groups = [[x * line + s for x in range(ka_count // line)] for s in range(line)]
    pieces = lax.all_to_all(pieces, "ka", 0, 0, axis_index_groups=near_groups, tiled=True)
    mv, mc, word = densities((here, ahead), False, zv, zc, None)
    rows = jnp.transpose(pieces, (1, 2, 0, 3, 4)).reshape(SLOTS, 2, 4 * line, 128)
    rows = rows + jnp.minimum(word[0, 0], 0).astype(bf16)
    w = lax.all_gather(rows, "ka", axis_index_groups=x_groups)
    ahead2 = from_behind(ahead, "ka", -2)
    behind2 = from_behind(behind, "ka", 2)
    mv, mc, words = densities((behind2, behind, here, ahead, ahead2), True, zv, zc, (mv, mc))
    order, slot_of, used = schedule(words[:, :PAIRS].reshape(TOTAL))
    partial = apply_screened(order, slot_of, used, ga_word, mv, mc, w)
    arrived = lax.ppermute(partial[2:].astype(bf16), "ga", [(0, 1), (1, 0), (2, 3), (3, 2)])
    both = partial[:2] + arrived.astype(f32)
    first_offset = ((lax.broadcasted_iota(jnp.int32, (1, 1, 1, 1, 128), 4) >> 5) & 1) == 0
    spread = lambda x, before, after: jnp.pad(x, ((0, 0), (before, after), (0, 0), (0, 0), (0, 0)))
    mirror = jnp.where(first_offset, spread(both[:, :, :, 24:], 1, 1), spread(both[:, :, :, 24:], 2, 0))
    parts = jnp.concatenate([spread(both[:, :, :, :24], 0, 2), mirror], axis=3)
    send = lambda picks, by: from_behind(jnp.stack([parts[:, d] for d in picks]).astype(bf16), "ka", by).astype(f32)
    plus_one = send((1, 5, 9), 1)
    plus_two = send((2, 6), 2)
    minus_one = send((3, 7), -1)
    low = parts[:, 0] + plus_one[0] + plus_two[0]
    high = parts[:, 8] + plus_one[2] + minus_one[1]
    total = parts[:, 4] + plus_one[1] + plus_two[1] + minus_one[0]
    total = total + from_behind(low, "ka", -4) + from_behind(high, "ka", 4)
    total = total[0] + lax.ppermute(total[1], "ga", [(0, 2), (2, 0), (1, 3), (3, 1)])
    return arrange(ga_word, total)


def solution(mesh):
    in_specs = (
        P("ka", None, None, None),
        P(None, None, "ga"),
        P(None, None, ("ga", "ka"), None),
        P("ka", None, None),
    )
    out_specs = P("ka", None, None, "ga")
    return jax.shard_map(body, mesh=mesh, in_specs=in_specs, out_specs=out_specs, check_vma=False)
```

```python
import functools
import jax
import jax.numpy as jnp
from jax import lax
from jax.experimental import pallas as pl
from jax.experimental.pallas import tpu as pltpu
from jax.sharding import PartitionSpec as P

f32 = jnp.float32
bf16 = jnp.bfloat16

WIN = 8
KB = 6
PAIRS = 72
TOTAL = WIN * PAIRS
CHUNK = 16
SLOTS = 22
UNROLL = 4
CHUNKS = (TOTAL + SLOTS * (CHUNK - 1)) // CHUNK // UNROLL * UNROLL + UNROLL
MSG = 112
VMEM_LIMIT = 50 * 2**20


def from_behind(x, axis, by):
    count = lax.axis_size(axis)
    return lax.ppermute(x, axis, [(i, (i + by) % count) for i in range(count)])


def half_swap(mask, first, second):
    return jnp.where(mask, first, pltpu.roll(second, 4, 0))


def density_kernel(count, rest, steps, *refs):
    pair_refs = refs[:count]
    zv_ref, zc_ref = refs[count : count + 2]
    mv_ref, mc_ref, slots_ref, left, right, va, ca, vb, cb = refs[-9:]
    step = pl.program_id(0)
    low = lax.broadcasted_iota(jnp.int32, (8, 1024), 0) < 4

    def produce(chunk, v_buf, c_buf):
        block = chunk // 3
        jh = chunk % 3
        if rest:
            block = block + jnp.where(block >= 2, 4, 0)
        for cv, buf in ((0, v_buf), (1, c_buf)):
            for jl in range(2):
                point = block * KB + 2 * jh + jl
                for part in range(4):
                    cols = slice(256 * part, 256 * part + 256)
                    imag_cols = slice(1024 + 256 * part, 1280 + 256 * part)
                    lefts = []
                    for band in range(4):
                        row = 4 * cv + band
                        lr = jnp.broadcast_to(left[point, row : row + 1, cols], (8, 256))
                        li = jnp.broadcast_to(left[point, 8 + row : 9 + row, cols], (8, 256))
                        lefts.append((lr, li))
                    for o in range(2):
                        for p in range(3):
                            rr = right[(block + o) * 3 + p, cv, 0, :, cols]
                            ri = right[(block + o) * 3 + p, cv, 1, :, cols]
                            base = ((jl * 2 + o) * 3 + p) * 32
                            for half in range(2):
                                reals = []
                                imags = []
                                for lr, li in lefts[2 * half : 2 * half + 2]:
                                    reals.append(lr * rr + li * ri)
                                    imags.append(lr * ri - li * rr)
                                rows = slice(base + 16 * half, base + 16 * half + 16)
                                buf[rows, cols] = jnp.concatenate(reals, axis=0).astype(bf16)
                                buf[rows, imag_cols] = jnp.concatenate(imags, axis=0).astype(bf16)
                    yield

    def consume(sub, v_buf, c_buf):
        mask = lax.broadcasted_iota(jnp.int32, (8, 256), 0) < 4
        for buf, z_ref, out_ref in ((v_buf, zv_ref, mv_ref), (c_buf, zc_ref, mc_ref)):
            for tile in range(z_ref.shape[1] // 256):
                cols = slice(256 * tile, 256 * tile + 256)
                for jl in range(2):
                    res = jnp.dot(buf[192 * jl : 192 * jl + 192], z_ref[:, cols], preferred_element_type=f32)
                    for o in range(2):
                        for p in range(3):
                            base = (o * 3 + p) * 32
                            a = [res[base + 8 * c : base + 8 * c + 8] for c in range(4)]
                            first = [half_swap(mask, a[0], a[1]), half_swap(mask, a[2], a[3])]
                            second = [
                                jnp.where(mask, pltpu.roll(a[0], 4, 0), a[1]),
                                jnp.where(mask, pltpu.roll(a[2], 4, 0), a[3]),
                            ]
                            for jj, value in ((0, first), (1, second)):
                                index = sub * 24 + (2 * p + jj) * 4 + jl * 2 + o
                                out_ref[index, :, cols] = jnp.concatenate(value, axis=0).astype(bf16)
                    yield

    def drain(*generators):
        live = list(generators)
        while live:
            live = [g for g in live if next(g, True) is None]

    @pl.when(step == 0)
    def _():
        for b in range(2 * count):
            if b < WIN:
                tail = pair_refs[b // 2][b % 2, 96:112, 0:128].astype(f32)
                slots_ref[b : b + 1, :] = tail[0:1].astype(jnp.int32)
            for j in range(KB):
                x = pair_refs[b // 2][b % 2, 16 * j : 16 * j + 16, :].astype(f32)
                left[b * KB + j] = x
                if b > 0:
                    index = (b - 1) * 3 + j // 2
                    for r in range(2):
                        half = x[8 * r : 8 * r + 8]
                        turned = pltpu.roll(half, 4, 0)
                        if j % 2 == 0:
                            right[index, 0, r] = half
                            right[index, 1, r] = turned
                        else:
                            right[index, 0, r] = jnp.where(low, right[index, 0, r], turned)
                            right[index, 1, r] = jnp.where(low, right[index, 1, r], half)
        drain(produce(0, va, ca))

    drain(consume(0, va, ca), produce(2 * step + 1, vb, cb))
    drain(consume(1, vb, cb), produce(jnp.minimum(2 * step + 2, 2 * steps - 1), va, ca))


def densities(pairs, rest, zv, zc, previous):
    whole = lambda shape: pl.BlockSpec(shape, lambda n: (0,) * len(shape), pipeline_mode=pl.Buffered(1))
    operands = list(pairs) + [zv, zc]
    in_specs = [whole(x.shape) for x in operands]
    aliases = {}
    if previous is not None:
        aliases = {len(operands): 0, len(operands) + 1: 1}
        in_specs += [pl.BlockSpec(memory_space=pl.ANY)] * 2
        operands += list(previous)
    count = len(pairs)
    steps = 6
    place = (lambda n: (n + jnp.where(n >= 3, 6, 0), 0, 0)) if rest else (lambda n: (3 + n, 0, 0))
    wv = zv.shape[1]
    wc = zc.shape[1]
    return pl.pallas_call(
        functools.partial(density_kernel, count, rest, steps),
        grid=(steps,),
        in_specs=in_specs,
        out_specs=[
            pl.BlockSpec((48, 16, wv), place),
            pl.BlockSpec((48, 16, wc), place),
            pl.BlockSpec((min(2 * count, WIN), 128), lambda n: (0, 0)),
        ],
        out_shape=[
            jax.ShapeDtypeStruct((TOTAL, 16, wv), bf16),
            jax.ShapeDtypeStruct((TOTAL, 16, wc), bf16),
            jax.ShapeDtypeStruct((min(2 * count, WIN), 128), jnp.int32),
        ],
        scratch_shapes=[
            pltpu.VMEM((2 * count * KB, 16, 1024), f32),
            pltpu.VMEM(((2 * count - 1) * 3, 2, 2, 8, 1024), f32),
            pltpu.VMEM((384, 2048), bf16),
            pltpu.VMEM((384, 2048), bf16),
            pltpu.VMEM((384, 2048), bf16),
            pltpu.VMEM((384, 2048), bf16),
        ],
        input_output_aliases=aliases,
        compiler_params=pltpu.CompilerParams(vmem_limit_bytes=VMEM_LIMIT),
        cost_estimate=pl.CostEstimate(
            flops=2 * steps * 48 * 16 * 2048 * (wv + wc), bytes_accessed=steps * 3 * 2**20, transcendentals=0
        ),
        name="densities",
    )(*operands)


def quarter_rows():
    own = [[(0, 0, 0, 16)], [(0, 16, 0, 8), (1, 0, 8, 8)], [(1, 8, 0, 16)]]
    own += [[(q + 2, r, s, n) for q, r, s, n in item] for item in own]
    mirror = [[(0, 24)], [(0, 40), (1, 24)], [(1, 40)]]
    mirror += [[(q + 2, r) for q, r in item] for item in mirror]
    return own, mirror


def apply_kernel(order_ref, slot_ref, used_ref, ga_ref, mv_hbm, mc_hbm, w_ref, out_ref, rhs, xv, mv_ref, mc_ref, done):
    fetch_v = pltpu.make_async_copy(mv_hbm, mv_ref, done.at[0])
    fetch_c = pltpu.make_async_copy(mc_hbm, mc_ref, done.at[1])
    fetch_v.start()
    fetch_c.start()
    ga = ga_ref[0]
    lane_group = lax.broadcasted_iota(jnp.int32, (16, 128), 1) >> 5
    spots = [(((q & 1) ^ (ga & 1)) << 1) | ((q >> 1) ^ (ga >> 1)) for q in range(4)]
    own_rows, mirror_rows = quarter_rows()

    def build(slot, carry):
        for x in range(4):
            wr = w_ref[x, slot, 0]
            wi = w_ref[x, slot, 1]
            rhs[slot, 64 * x : 64 * x + 64, 0:128] = wr
            rhs[slot, 64 * x : 64 * x + 64, 128:256] = -wi
            rhs[slot, 256 + 64 * x : 320 + 64 * x, 0:128] = wi
            rhs[slot, 256 + 64 * x : 320 + 64 * x, 128:256] = wr
        return carry

    lax.fori_loop(0, SLOTS, build, 0)
    fetch_v.wait()

    def chunk(q, carry):
        for u in range(UNROLL):
            slot = slot_ref[UNROLL * q + u]
            ids = [order_ref[(UNROLL * q + u) * CHUNK + i] for i in range(CHUNK)]
            sources = [jnp.minimum(i, TOTAL - 1) for i in ids]
            lhs = jnp.concatenate([mv_ref[s] for s in sources], axis=0)
            res = jnp.dot(lhs, rhs[slot], preferred_element_type=f32).astype(bf16)
            for i in range(CHUNK):
                xv[ids[i]] = res[16 * i : 16 * i + 16]
        return carry

    lax.fori_loop(0, (used_ref[0] + UNROLL - 1) >> 2, chunk, 0)
    fetch_c.wait()

    def contract(t, carry):
        for jh in range(3):
            for h in range(3):
                first = ((t * 3 + jh) * 6 + 2 * h) * 4
                rows = []
                for i in range(8):
                    y = mc_ref[first + i]
                    rows.append(y)
                    rows.append(jnp.concatenate([-y[:, 128:], y[:, :128]], axis=1))
                lhs = jnp.concatenate([xv[first + i] for i in range(8)], axis=0)
                d = lax.dot_general(
                    lhs, jnp.concatenate(rows, axis=0), (((1,), (1,)), ((), ())), preferred_element_type=f32
                )
                blocks = [
                    [d[16 * i : 16 * i + 16, 128 * (i // 4) : 128 * (i // 4) + 128] for i in range(4 * l, 4 * l + 4)]
                    for l in range(2)
                ]
                odd = (lane_group & 1) == 1
                low = lane_group < 2
                mixed = [[jnp.where(odd, b[2 * jl + 1], b[2 * jl]) for jl in range(2)] for b in blocks]
                for l in range(2):
                    own = jnp.where(low, mixed[l][0], mixed[l][1])
                    for q, r, s, n in own_rows[2 * h + l]:
                        out_ref[spots[q], t, jh, r : r + n, :] = own[s : s + n]
                for jl in range(2):
                    if jl == 0:
                        mirror = jnp.where(low, mixed[0][0], pltpu.roll(mixed[1][0], 64, 1))
                    else:
                        mirror = jnp.where(low, pltpu.roll(mixed[0][1], 64, 1), mixed[1][1])
                    for q, r in mirror_rows[2 * jh + jl]:
                        out_ref[spots[q], t, h, r : r + 16, :] = mirror
        return carry

    lax.fori_loop(0, WIN, contract, 0)


def apply_screened(order, slots, used, ga, mv, mc, w):
    smem = pl.BlockSpec(memory_space=pltpu.SMEM)
    vmem = pl.BlockSpec(memory_space=pltpu.VMEM)
    return pl.pallas_call(
        apply_kernel,
        in_specs=[smem] * 4 + [pl.BlockSpec(memory_space=pl.ANY)] * 2 + [vmem],
        out_specs=vmem,
        out_shape=jax.ShapeDtypeStruct((4, WIN, 3, 56, 128), f32),
        scratch_shapes=[
            pltpu.VMEM((SLOTS, 512, 256), bf16),
            pltpu.VMEM((TOTAL + 1, 16, 256), bf16),
            pltpu.VMEM(mv.shape, bf16),
            pltpu.VMEM(mc.shape, bf16),
            pltpu.SemaphoreType.DMA((2,)),
        ],
        compiler_params=pltpu.CompilerParams(vmem_limit_bytes=VMEM_LIMIT),
        cost_estimate=pl.CostEstimate(flops=6 * 10**9, bytes_accessed=18 * 2**20, transcendentals=0),
        name="apply_screened",
    )(order, slots, used, ga, mv, mc, w)


def split_dot(x, sel):
    high = x.astype(bf16)
    low = (x - high.astype(f32)).astype(bf16)
    return jnp.dot(high, sel, preferred_element_type=f32) + jnp.dot(low, sel, preferred_element_type=f32)


def arrange_kernel(ga_ref, parts_ref, out_ref):
    ga = ga_ref[0]
    src = lax.broadcasted_iota(jnp.int32, (128, 384), 0)
    lane = lax.broadcasted_iota(jnp.int32, (128, 384), 1)
    row = lax.broadcasted_iota(jnp.int32, (32, 384), 0)
    row_lane = lax.broadcasted_iota(jnp.int32, (32, 384), 1)
    start = ga + (ga >> 1)
    outer = row_lane >> 6
    place = 6 * ga + outer
    own = (24, (lane >> 4) & 3, lane & 3, outer * 4 + ((row_lane >> 2) & 3))
    mirror = (32, lane & 3, (lane >> 4) & 3, ((place >> 2) - start) * 16 + ((row_lane >> 2) & 3) * 4 + (place & 3))
    for kind, (count, c, c2, wanted) in enumerate((own, mirror)):
        low = 24 * kind
        x = jnp.concatenate([parts_ref[jh, low : low + count, :] for jh in range(3)], axis=0)
        keep = row[:count] == wanted[:count]
        for combo in range(8):
            sel = (src == combo * 16 + c * 4 + c2).astype(f32).astype(bf16)
            spread = split_dot(x, sel)
            for jh in range(3):
                rows = spread[count * jh : count * jh + count]
                picked = jnp.sum(jnp.where(keep, rows, 0.0), axis=0, keepdims=True)
                if kind == 1 and combo % 2 == 1:
                    picked = -picked
                out_ref[2 * jh + combo // 4, 2 * kind + (combo // 2) % 2, pl.ds(combo % 2, 1), :] = picked


def arrange(ga, parts):
    vmem = pl.BlockSpec(memory_space=pltpu.VMEM)
    return pl.pallas_call(
        arrange_kernel,
        in_specs=[pl.BlockSpec(memory_space=pltpu.SMEM), vmem],
        out_specs=vmem,
        out_shape=jax.ShapeDtypeStruct((KB, 4, 2, 384), f32),
        compiler_params=pltpu.CompilerParams(vmem_limit_bytes=VMEM_LIMIT),
        name="arrange",
    )(ga, parts)


def schedule(slots):
    pair = jnp.arange(TOTAL, dtype=jnp.int32)
    names = jnp.arange(SLOTS, dtype=jnp.int32)
    hot = slots[:, None] == names[None, :]
    needed = (jnp.sum(hot.astype(jnp.int32), axis=0) + CHUNK - 1) // CHUNK
    start = jnp.sum(jnp.where(names[:, None] < names[None, :], needed[:, None], 0), axis=0)
    same = (slots[:, None] == slots[None, :]) & (pair[None, :] < pair[:, None])
    rank = jnp.sum(same.astype(jnp.int32), axis=1)
    place = jnp.sum(jnp.where(hot, start[None, :], 0), axis=1) * CHUNK + rank
    seat = jnp.arange(CHUNKS * CHUNK, dtype=jnp.int32)
    taken = place[None, :] == seat[:, None]
    order = TOTAL + jnp.sum(jnp.where(taken, pair[None, :] - TOTAL, 0), axis=1)
    chunk = jnp.arange(CHUNKS, dtype=jnp.int32)
    ended = (start + needed)[None, :] <= chunk[:, None]
    slot_of = jnp.minimum(jnp.sum(ended.astype(jnp.int32), axis=1), SLOTS - 1)
    return order, slot_of, jnp.sum(needed).reshape(1)


def zeta_matrix(zeta):
    zr = zeta[:, 0]
    zi = zeta[:, 1]
    return jnp.concatenate([jnp.concatenate([zr, zi], axis=1), jnp.concatenate([-zi, zr], axis=1)], axis=0)


def body(bloch_samples, zeta_vectors, screened, pair_slots):
    ka_count = lax.axis_size("ka")
    ka = lax.axis_index("ka")
    ga = lax.axis_index("ga")
    ga_word = ga.reshape(1).astype(jnp.int32)
    part = lax.rem(ka, WIN)
    slots = jnp.transpose(pair_slots.reshape(3, 2, 2, KB), (0, 3, 1, 2)).reshape(1, PAIRS)
    tail = jnp.pad(slots.astype(bf16), ((0, 15), (0, 1024 - PAIRS)))
    message = jnp.concatenate([bloch_samples.reshape(96, 1024), tail], axis=0)
    following = from_behind(message, "ka", -1)
    here = jnp.stack([message, following])
    ahead = from_behind(here, "ka", -2)
    behind = from_behind(here, "ka", 2)
    zv = zeta_matrix(zeta_vectors)
    mine = lax.dynamic_slice_in_dim(zeta_vectors, 128 * lax.rem(part, 2), 128, 2)
    halves = lax.all_gather(mine, "ga")
    zc = zeta_matrix(lax.dynamic_index_in_dim(halves, part // 2, 0, keepdims=False))
    pieces = jnp.transpose(screened.reshape(SLOTS, 2, 4, WIN, 128), (3, 0, 1, 2, 4))
    pieces = jnp.concatenate([pieces, pieces], axis=0)
    line = 2 * WIN
    near_groups = [[x * line + s for s in range(line)] for x in range(ka_count // line)]
    x_groups = [[x * line + s for x in range(ka_count // line)] for s in range(line)]
    pieces = lax.all_to_all(pieces, "ka", 0, 0, axis_index_groups=near_groups, tiled=True)
    rows = jnp.transpose(pieces, (1, 2, 0, 3, 4)).reshape(SLOTS, 2, 4 * line, 128)
    w = lax.all_gather(rows, "ka", axis_index_groups=x_groups)
    ahead2 = from_behind(ahead, "ka", -2)
    behind2 = from_behind(behind, "ka", 2)
    mv, mc, _ = densities((behind, here, ahead), False, zv, zc, None)
    mv, mc, words = densities((behind2, behind, here, ahead, ahead2), True, zv, zc, (mv, mc))
    order, slot_of, used = schedule(words[:, :PAIRS].reshape(TOTAL))
    partial = apply_screened(order, slot_of, used, ga_word, mv, mc, w)
    arrived = lax.ppermute(partial[2:].astype(bf16), "ga", [(0, 1), (1, 0), (2, 3), (3, 2)])
    own = partial[0] + arrived[0].astype(f32)
    other = (partial[1] + arrived[1].astype(f32)).astype(bf16)
    own = own + lax.ppermute(other, "ga", [(0, 2), (2, 0), (1, 3), (3, 1)]).astype(f32)
    first_offset = ((lax.broadcasted_iota(jnp.int32, (1, 1, 1, 128), 3) >> 5) & 1) == 0
    spread = lambda x, before, after: jnp.pad(x, ((before, after), (0, 0), (0, 0), (0, 0)))
    mirror = jnp.where(first_offset, spread(own[:, :, 24:], 1, 1), spread(own[:, :, 24:], 2, 0))
    parts = jnp.concatenate([spread(own[:, :, :24], 0, 2), mirror], axis=2)
    send = lambda picks, by: from_behind(jnp.stack([parts[d] for d in picks]).astype(bf16), "ka", by).astype(f32)
    plus_one = send((1, 5, 9), 1)
    plus_two = send((2, 6), 2)
    minus_one = send((3, 7), -1)
    low = parts[0] + plus_one[0] + plus_two[0]
    high = parts[8] + plus_one[2] + minus_one[1]
    total = parts[4] + plus_one[1] + plus_two[1] + minus_one[0]
    total = total + from_behind(low, "ka", -4) + from_behind(high, "ka", 4)
    return arrange(ga_word, total)


def solution(mesh):
    in_specs = (
        P("ka", None, None, None),
        P(None, None, "ga"),
        P(None, None, ("ga", "ka"), None),
        P("ka", None, None),
    )
    out_specs = P("ka", None, None, "ga")
    return jax.shard_map(body, mesh=mesh, in_specs=in_specs, out_specs=out_specs, check_vma=False)
```

```python
import functools
import jax
import jax.numpy as jnp
from jax import lax
from jax.experimental import pallas as pl
from jax.experimental.pallas import tpu as pltpu
from jax.sharding import PartitionSpec as P

f32 = jnp.float32
bf16 = jnp.bfloat16

WIN = 8
KB = 6
PAIRS = 72
TOTAL = WIN * PAIRS
CHUNK = 16
SLOTS = 22
UNROLL = 4
CHUNKS = (TOTAL + SLOTS * (CHUNK - 1)) // CHUNK // UNROLL * UNROLL + UNROLL
MSG = 112
VMEM_LIMIT = 50 * 2**20


def from_behind(x, axis, by):
    count = lax.axis_size(axis)
    return lax.ppermute(x, axis, [(i, (i + by) % count) for i in range(count)])


def half_swap(mask, first, second):
    return jnp.where(mask, first, pltpu.roll(second, 4, 0))


def density_kernel(count, rest, steps, *refs):
    pair_refs = refs[:count]
    zv_ref, zc_ref = refs[count : count + 2]
    mv_ref, mc_ref, slots_ref, left, right, va, ca, vb, cb = refs[-9:]
    step = pl.program_id(0)
    low = lax.broadcasted_iota(jnp.int32, (8, 1024), 0) < 4

    def produce(chunk, v_buf, c_buf):
        block = chunk // 3
        jh = chunk % 3
        if rest:
            block = block + jnp.where(block >= 2, 4, 0)
        for cv, buf in ((0, v_buf), (1, c_buf)):
            for jl in range(2):
                point = block * KB + 2 * jh + jl
                for part in range(4):
                    cols = slice(256 * part, 256 * part + 256)
                    imag_cols = slice(1024 + 256 * part, 1280 + 256 * part)
                    lefts = []
                    for band in range(4):
                        row = 4 * cv + band
                        lr = jnp.broadcast_to(left[point, row : row + 1, cols], (8, 256))
                        li = jnp.broadcast_to(left[point, 8 + row : 9 + row, cols], (8, 256))
                        lefts.append((lr, li))
                    for o in range(2):
                        for p in range(3):
                            rr = right[(block + o) * 3 + p, cv, 0, :, cols]
                            ri = right[(block + o) * 3 + p, cv, 1, :, cols]
                            base = ((jl * 2 + o) * 3 + p) * 32
                            for half in range(2):
                                reals = []
                                imags = []
                                for lr, li in lefts[2 * half : 2 * half + 2]:
                                    reals.append(lr * rr + li * ri)
                                    imags.append(lr * ri - li * rr)
                                rows = slice(base + 16 * half, base + 16 * half + 16)
                                buf[rows, cols] = jnp.concatenate(reals, axis=0).astype(bf16)
                                buf[rows, imag_cols] = jnp.concatenate(imags, axis=0).astype(bf16)
                    yield

    def consume(sub, v_buf, c_buf):
        mask = lax.broadcasted_iota(jnp.int32, (8, 256), 0) < 4
        for buf, z_ref, out_ref in ((v_buf, zv_ref, mv_ref), (c_buf, zc_ref, mc_ref)):
            for tile in range(z_ref.shape[1] // 256):
                cols = slice(256 * tile, 256 * tile + 256)
                res = jnp.dot(buf[...], z_ref[:, cols], preferred_element_type=f32)
                yield
                for group in range(12):
                    base = group * 32
                    jl, o, p = group // 6, group // 3 % 2, group % 3
                    a = [res[base + 8 * c : base + 8 * c + 8] for c in range(4)]
                    first = [half_swap(mask, a[0], a[1]), half_swap(mask, a[2], a[3])]
                    second = [
                        jnp.where(mask, pltpu.roll(a[0], 4, 0), a[1]),
                        jnp.where(mask, pltpu.roll(a[2], 4, 0), a[3]),
                    ]
                    for jj, value in ((0, first), (1, second)):
                        index = sub * 24 + (2 * p + jj) * 4 + jl * 2 + o
                        out_ref[index, :, cols] = jnp.concatenate(value, axis=0).astype(bf16)

    def together(matmuls, products):
        for _ in matmuls:
            for _ in range(6):
                next(products, None)
        for _ in products:
            pass

    @pl.when(step == 0)
    def _():
        for b in range(2 * count):
            if b < WIN:
                tail = pair_refs[b // 2][b % 2, 96:112, 0:128].astype(f32)
                slots_ref[b : b + 1, :] = tail[0:1].astype(jnp.int32)
            for j in range(KB):
                x = pair_refs[b // 2][b % 2, 16 * j : 16 * j + 16, :].astype(f32)
                left[b * KB + j] = x
                if b > 0:
                    index = (b - 1) * 3 + j // 2
                    for r in range(2):
                        half = x[8 * r : 8 * r + 8]
                        turned = pltpu.roll(half, 4, 0)
                        if j % 2 == 0:
                            right[index, 0, r] = half
                            right[index, 1, r] = turned
                        else:
                            right[index, 0, r] = jnp.where(low, right[index, 0, r], turned)
                            right[index, 1, r] = jnp.where(low, right[index, 1, r], half)
        together((), produce(0, va, ca))

    together(consume(0, va, ca), produce(2 * step + 1, vb, cb))
    together(consume(1, vb, cb), produce(jnp.minimum(2 * step + 2, 2 * steps - 1), va, ca))


def densities(pairs, rest, zv, zc, previous):
    whole = lambda shape: pl.BlockSpec(shape, lambda n: (0,) * len(shape), pipeline_mode=pl.Buffered(1))
    operands = list(pairs) + [zv, zc]
    in_specs = [whole(x.shape) for x in operands]
    aliases = {}
    if previous is not None:
        aliases = {len(operands): 0, len(operands) + 1: 1}
        in_specs += [pl.BlockSpec(memory_space=pl.ANY)] * 2
        operands += list(previous)
    count = len(pairs)
    steps = 6
    place = (lambda n: (n + jnp.where(n >= 3, 6, 0), 0, 0)) if rest else (lambda n: (3 + n, 0, 0))
    wv = zv.shape[1]
    wc = zc.shape[1]
    return pl.pallas_call(
        functools.partial(density_kernel, count, rest, steps),
        grid=(steps,),
        in_specs=in_specs,
        out_specs=[
            pl.BlockSpec((48, 16, wv), place),
            pl.BlockSpec((48, 16, wc), place),
            pl.BlockSpec((min(2 * count, WIN), 128), lambda n: (0, 0)),
        ],
        out_shape=[
            jax.ShapeDtypeStruct((TOTAL, 16, wv), bf16),
            jax.ShapeDtypeStruct((TOTAL, 16, wc), bf16),
            jax.ShapeDtypeStruct((min(2 * count, WIN), 128), jnp.int32),
        ],
        scratch_shapes=[
            pltpu.VMEM((2 * count * KB, 16, 1024), f32),
            pltpu.VMEM(((2 * count - 1) * 3, 2, 2, 8, 1024), f32),
            pltpu.VMEM((384, 2048), bf16),
            pltpu.VMEM((384, 2048), bf16),
            pltpu.VMEM((384, 2048), bf16),
            pltpu.VMEM((384, 2048), bf16),
        ],
        input_output_aliases=aliases,
        compiler_params=pltpu.CompilerParams(vmem_limit_bytes=VMEM_LIMIT),
        cost_estimate=pl.CostEstimate(
            flops=2 * steps * 48 * 16 * 2048 * (wv + wc), bytes_accessed=steps * 3 * 2**20, transcendentals=0
        ),
        name="densities",
    )(*operands)


def quarter_rows():
    own = [[(0, 0, 0, 16)], [(0, 16, 0, 8), (1, 0, 8, 8)], [(1, 8, 0, 16)]]
    own += [[(q + 2, r, s, n) for q, r, s, n in item] for item in own]
    mirror = [[(0, 24)], [(0, 40), (1, 24)], [(1, 40)]]
    mirror += [[(q + 2, r) for q, r in item] for item in mirror]
    return own, mirror


def apply_kernel(order_ref, slot_ref, used_ref, ga_ref, mv_hbm, mc_hbm, w_ref, out_ref, rhs, xv, mv_ref, mc_ref, done):
    fetch_v = pltpu.make_async_copy(mv_hbm, mv_ref, done.at[0])
    fetch_c = pltpu.make_async_copy(mc_hbm, mc_ref, done.at[1])
    fetch_v.start()
    ga = ga_ref[0]
    lane_group = lax.broadcasted_iota(jnp.int32, (16, 128), 1) >> 5
    spots = [(((q & 1) ^ (ga & 1)) << 1) | ((q >> 1) ^ (ga >> 1)) for q in range(4)]
    own_rows, mirror_rows = quarter_rows()

    def build(slot, carry):
        for x in range(4):
            wr = w_ref[x, slot, 0]
            wi = w_ref[x, slot, 1]
            rhs[slot, 64 * x : 64 * x + 64, 0:128] = wr
            rhs[slot, 64 * x : 64 * x + 64, 128:256] = -wi
            rhs[slot, 256 + 64 * x : 320 + 64 * x, 0:128] = wi
            rhs[slot, 256 + 64 * x : 320 + 64 * x, 128:256] = wr
        return carry

    lax.fori_loop(0, SLOTS, build, 0)
    fetch_v.wait()
    fetch_c.start()

    def chunk(q, carry):
        for u in range(UNROLL):
            slot = slot_ref[UNROLL * q + u]
            ids = [order_ref[(UNROLL * q + u) * CHUNK + i] for i in range(CHUNK)]
            sources = [jnp.minimum(i, TOTAL - 1) for i in ids]
            lhs = jnp.concatenate([mv_ref[s] for s in sources], axis=0)
            res = jnp.dot(lhs, rhs[slot], preferred_element_type=f32).astype(bf16)
            for i in range(CHUNK):
                xv[ids[i]] = res[16 * i : 16 * i + 16]
        return carry

    lax.fori_loop(0, (used_ref[0] + UNROLL - 1) >> 2, chunk, 0)
    fetch_c.wait()

    def contract(t, carry):
        for jh in range(3):
            for h in range(3):
                first = ((t * 3 + jh) * 6 + 2 * h) * 4
                rows = []
                for i in range(8):
                    y = mc_ref[first + i]
                    rows.append(y)
                    rows.append(jnp.concatenate([-y[:, 128:], y[:, :128]], axis=1))
                lhs = jnp.concatenate([xv[first + i] for i in range(8)], axis=0)
                d = lax.dot_general(
                    lhs, jnp.concatenate(rows, axis=0), (((1,), (1,)), ((), ())), preferred_element_type=f32
                )
                blocks = [
                    [d[16 * i : 16 * i + 16, 128 * (i // 4) : 128 * (i // 4) + 128] for i in range(4 * l, 4 * l + 4)]
                    for l in range(2)
                ]
                odd = (lane_group & 1) == 1
                low = lane_group < 2
                mixed = [[jnp.where(odd, b[2 * jl + 1], b[2 * jl]) for jl in range(2)] for b in blocks]
                for l in range(2):
                    own = jnp.where(low, mixed[l][0], mixed[l][1])
                    for q, r, s, n in own_rows[2 * h + l]:
                        out_ref[spots[q], t, jh, r : r + n, :] = own[s : s + n]
                for jl in range(2):
                    if jl == 0:
                        mirror = jnp.where(low, mixed[0][0], pltpu.roll(mixed[1][0], 64, 1))
                    else:
                        mirror = jnp.where(low, pltpu.roll(mixed[0][1], 64, 1), mixed[1][1])
                    for q, r in mirror_rows[2 * jh + jl]:
                        out_ref[spots[q], t, h, r : r + 16, :] = mirror
        return carry

    lax.fori_loop(0, WIN, contract, 0)


def apply_screened(order, slots, used, ga, mv, mc, w):
    smem = pl.BlockSpec(memory_space=pltpu.SMEM)
    vmem = pl.BlockSpec(memory_space=pltpu.VMEM)
    return pl.pallas_call(
        apply_kernel,
        in_specs=[smem] * 4 + [pl.BlockSpec(memory_space=pl.ANY)] * 2 + [vmem],
        out_specs=vmem,
        out_shape=jax.ShapeDtypeStruct((4, WIN, 3, 56, 128), f32),
        scratch_shapes=[
            pltpu.VMEM((SLOTS, 512, 256), bf16),
            pltpu.VMEM((TOTAL + 1, 16, 256), bf16),
            pltpu.VMEM(mv.shape, bf16),
            pltpu.VMEM(mc.shape, bf16),
            pltpu.SemaphoreType.DMA((2,)),
        ],
        compiler_params=pltpu.CompilerParams(vmem_limit_bytes=VMEM_LIMIT),
        cost_estimate=pl.CostEstimate(flops=6 * 10**9, bytes_accessed=18 * 2**20, transcendentals=0),
        name="apply_screened",
    )(order, slots, used, ga, mv, mc, w)


def split_dot(x, sel):
    high = x.astype(bf16)
    low = (x - high.astype(f32)).astype(bf16)
    return jnp.dot(high, sel, preferred_element_type=f32) + jnp.dot(low, sel, preferred_element_type=f32)


def arrange_kernel(ga_ref, parts_ref, out_ref):
    ga = ga_ref[0]
    src = lax.broadcasted_iota(jnp.int32, (128, 384), 0)
    lane = lax.broadcasted_iota(jnp.int32, (128, 384), 1)
    row = lax.broadcasted_iota(jnp.int32, (32, 384), 0)
    row_lane = lax.broadcasted_iota(jnp.int32, (32, 384), 1)
    start = ga + (ga >> 1)
    outer = row_lane >> 6
    place = 6 * ga + outer
    own = (24, (lane >> 4) & 3, lane & 3, outer * 4 + ((row_lane >> 2) & 3))
    mirror = (32, lane & 3, (lane >> 4) & 3, ((place >> 2) - start) * 16 + ((row_lane >> 2) & 3) * 4 + (place & 3))
    for kind, (count, c, c2, wanted) in enumerate((own, mirror)):
        low = 24 * kind
        x = jnp.concatenate([parts_ref[jh, low : low + count, :] for jh in range(3)], axis=0)
        keep = row[:count] == wanted[:count]
        for combo in range(8):
            sel = (src == combo * 16 + c * 4 + c2).astype(f32).astype(bf16)
            spread = split_dot(x, sel)
            for jh in range(3):
                rows = spread[count * jh : count * jh + count]
                picked = jnp.sum(jnp.where(keep, rows, 0.0), axis=0, keepdims=True)
                if kind == 1 and combo % 2 == 1:
                    picked = -picked
                out_ref[2 * jh + combo // 4, 2 * kind + (combo // 2) % 2, pl.ds(combo % 2, 1), :] = picked


def arrange(ga, parts):
    vmem = pl.BlockSpec(memory_space=pltpu.VMEM)
    return pl.pallas_call(
        arrange_kernel,
        in_specs=[pl.BlockSpec(memory_space=pltpu.SMEM), vmem],
        out_specs=vmem,
        out_shape=jax.ShapeDtypeStruct((KB, 4, 2, 384), f32),
        compiler_params=pltpu.CompilerParams(vmem_limit_bytes=VMEM_LIMIT),
        name="arrange",
    )(ga, parts)


def schedule(slots):
    pair = jnp.arange(TOTAL, dtype=jnp.int32)
    names = jnp.arange(SLOTS, dtype=jnp.int32)
    hot = slots[:, None] == names[None, :]
    needed = (jnp.sum(hot.astype(jnp.int32), axis=0) + CHUNK - 1) // CHUNK
    start = jnp.sum(jnp.where(names[:, None] < names[None, :], needed[:, None], 0), axis=0)
    same = (slots[:, None] == slots[None, :]) & (pair[None, :] < pair[:, None])
    rank = jnp.sum(same.astype(jnp.int32), axis=1)
    place = jnp.sum(jnp.where(hot, start[None, :], 0), axis=1) * CHUNK + rank
    seat = jnp.arange(CHUNKS * CHUNK, dtype=jnp.int32)
    taken = place[None, :] == seat[:, None]
    order = TOTAL + jnp.sum(jnp.where(taken, pair[None, :] - TOTAL, 0), axis=1)
    chunk = jnp.arange(CHUNKS, dtype=jnp.int32)
    ended = (start + needed)[None, :] <= chunk[:, None]
    slot_of = jnp.minimum(jnp.sum(ended.astype(jnp.int32), axis=1), SLOTS - 1)
    return order, slot_of, jnp.sum(needed).reshape(1)


def zeta_matrix(zeta):
    zr = zeta[:, 0]
    zi = zeta[:, 1]
    return jnp.concatenate([jnp.concatenate([zr, zi], axis=1), jnp.concatenate([-zi, zr], axis=1)], axis=0)


def body(bloch_samples, zeta_vectors, screened, pair_slots):
    ka_count = lax.axis_size("ka")
    ka = lax.axis_index("ka")
    ga = lax.axis_index("ga")
    ga_word = ga.reshape(1).astype(jnp.int32)
    part = lax.rem(ka, WIN)
    slots = jnp.transpose(pair_slots.reshape(3, 2, 2, KB), (0, 3, 1, 2)).reshape(1, PAIRS)
    tail = jnp.pad(slots.astype(bf16), ((0, 15), (0, 1024 - PAIRS)))
    message = jnp.concatenate([bloch_samples.reshape(96, 1024), tail], axis=0)
    following = from_behind(message, "ka", -1)
    here = jnp.stack([message, following])
    ahead = from_behind(here, "ka", -2)
    behind = from_behind(here, "ka", 2)
    zv = zeta_matrix(zeta_vectors)
    mine = lax.dynamic_slice_in_dim(zeta_vectors, 128 * lax.rem(part, 2), 128, 2)
    halves = lax.all_gather(mine, "ga")
    zc = zeta_matrix(lax.dynamic_index_in_dim(halves, part // 2, 0, keepdims=False))
    pieces = jnp.transpose(screened.reshape(SLOTS, 2, 4, WIN, 128), (3, 0, 1, 2, 4))
    pieces = jnp.concatenate([pieces, pieces], axis=0)
    pieces = pieces + message[0, 0] * 0
    line = 2 * WIN
    near_groups = [[x * line + s for s in range(line)] for x in range(ka_count // line)]
    x_groups = [[x * line + s for x in range(ka_count // line)] for s in range(line)]
    pieces = lax.all_to_all(pieces, "ka", 0, 0, axis_index_groups=near_groups, tiled=True)
    rows = jnp.transpose(pieces, (1, 2, 0, 3, 4)).reshape(SLOTS, 2, 4 * line, 128)
    w = lax.all_gather(rows, "ka", axis_index_groups=x_groups)
    zero = rows[0, 0, 0, 0] * 0
    ahead2 = from_behind(ahead + zero, "ka", -2)
    behind2 = from_behind(behind + zero, "ka", 2)
    mv, mc, _ = densities((behind, here, ahead), False, zv, zc, None)
    mv, mc, words = densities((behind2, behind, here, ahead, ahead2), True, zv, zc, (mv, mc))
    order, slot_of, used = schedule(words[:, :PAIRS].reshape(TOTAL))
    partial = apply_screened(order, slot_of, used, ga_word, mv, mc, w)
    arrived = lax.ppermute(partial[2:].astype(bf16), "ga", [(0, 1), (1, 0), (2, 3), (3, 2)])
    own = partial[0] + arrived[0].astype(f32)
    other = (partial[1] + arrived[1].astype(f32)).astype(bf16)
    own = own + lax.ppermute(other, "ga", [(0, 2), (2, 0), (1, 3), (3, 1)]).astype(f32)
    first_offset = ((lax.broadcasted_iota(jnp.int32, (1, 1, 1, 128), 3) >> 5) & 1) == 0
    spread = lambda x, before, after: jnp.pad(x, ((before, after), (0, 0), (0, 0), (0, 0)))
    mirror = jnp.where(first_offset, spread(own[:, :, 24:], 1, 1), spread(own[:, :, 24:], 2, 0))
    parts = jnp.concatenate([spread(own[:, :, :24], 0, 2), mirror], axis=2)
    send = lambda picks, by: from_behind(jnp.stack([parts[d] for d in picks]).astype(bf16), "ka", by).astype(f32)
    plus_one = send((1, 5, 9), 1)
    plus_two = send((2, 6), 2)
    minus_one = send((3, 7), -1)
    low = parts[0] + plus_one[0] + plus_two[0]
    high = parts[8] + plus_one[2] + minus_one[1]
    total = parts[4] + plus_one[1] + plus_two[1] + minus_one[0]
    total = total + from_behind(low, "ka", -4) + from_behind(high, "ka", 4)
    return arrange(ga_word, total)


def solution(mesh):
    in_specs = (
        P("ka", None, None, None),
        P(None, None, "ga"),
        P(None, None, ("ga", "ka"), None),
        P("ka", None, None),
    )
    out_specs = P("ka", None, None, "ga")
    return jax.shard_map(body, mesh=mesh, in_specs=in_specs, out_specs=out_specs, check_vma=False)
```

```python
import functools
import jax
import jax.numpy as jnp
from jax import lax
from jax.experimental import pallas as pl
from jax.experimental.pallas import tpu as pltpu
from jax.sharding import PartitionSpec as P

f32 = jnp.float32
bf16 = jnp.bfloat16

WIN = 8
KB = 6
PAIRS = 72
TOTAL = WIN * PAIRS
CHUNK = 16
SLOTS = 22
UNROLL = 4
CHUNKS = (TOTAL + SLOTS * (CHUNK - 1)) // CHUNK // UNROLL * UNROLL + UNROLL
MSG = 112
VMEM_LIMIT = 50 * 2**20


def from_behind(x, axis, by):
    count = lax.axis_size(axis)
    return lax.ppermute(x, axis, [(i, (i + by) % count) for i in range(count)])


def half_swap(mask, first, second):
    return jnp.where(mask, first, pltpu.roll(second, 4, 0))


def density_kernel(count, steps, *refs):
    pair_refs = refs[:count]
    zv_ref, zc_ref = refs[count : count + 2]
    mv_ref, mc_ref, slots_ref, left, right, va, ca, vb, cb = refs[-9:]
    step = pl.program_id(0)
    low = lax.broadcasted_iota(jnp.int32, (8, 1024), 0) < 4

    def produce(chunk, v_buf, c_buf):
        block = chunk // 3
        jh = chunk % 3
        for cv, buf in ((0, v_buf), (1, c_buf)):
            for jl in range(2):
                point = block * KB + 2 * jh + jl
                for part in range(4):
                    cols = slice(256 * part, 256 * part + 256)
                    imag_cols = slice(1024 + 256 * part, 1280 + 256 * part)
                    lefts = []
                    for band in range(4):
                        row = 4 * cv + band
                        lr = jnp.broadcast_to(left[point, row : row + 1, cols], (8, 256))
                        li = jnp.broadcast_to(left[point, 8 + row : 9 + row, cols], (8, 256))
                        lefts.append((lr, li))
                    for o in range(2):
                        for p in range(3):
                            rr = right[(block + o) * 3 + p, cv, 0, :, cols]
                            ri = right[(block + o) * 3 + p, cv, 1, :, cols]
                            base = ((jl * 2 + o) * 3 + p) * 32
                            for half in range(2):
                                reals = []
                                imags = []
                                for lr, li in lefts[2 * half : 2 * half + 2]:
                                    reals.append(lr * rr + li * ri)
                                    imags.append(lr * ri - li * rr)
                                rows = slice(base + 16 * half, base + 16 * half + 16)
                                buf[rows, cols] = jnp.concatenate(reals, axis=0).astype(bf16)
                                buf[rows, imag_cols] = jnp.concatenate(imags, axis=0).astype(bf16)
                    yield

    def consume(sub, v_buf, c_buf):
        mask = lax.broadcasted_iota(jnp.int32, (8, 256), 0) < 4
        for buf, z_ref, out_ref in ((v_buf, zv_ref, mv_ref), (c_buf, zc_ref, mc_ref)):
            for tile in range(z_ref.shape[1] // 256):
                cols = slice(256 * tile, 256 * tile + 256)
                res = jnp.dot(buf[...], z_ref[:, cols], preferred_element_type=f32)
                yield
                for group in range(12):
                    base = group * 32
                    jl, o, p = group // 6, group // 3 % 2, group % 3
                    a = [res[base + 8 * c : base + 8 * c + 8] for c in range(4)]
                    first = [half_swap(mask, a[0], a[1]), half_swap(mask, a[2], a[3])]
                    second = [
                        jnp.where(mask, pltpu.roll(a[0], 4, 0), a[1]),
                        jnp.where(mask, pltpu.roll(a[2], 4, 0), a[3]),
                    ]
                    for jj, value in ((0, first), (1, second)):
                        index = sub * 24 + (2 * p + jj) * 4 + jl * 2 + o
                        out_ref[index, :, cols] = jnp.concatenate(value, axis=0).astype(bf16)

    def together(matmuls, products):
        for _ in matmuls:
            for _ in range(6):
                next(products, None)
        for _ in products:
            pass

    @pl.when(step == 0)
    def _():
        for b in range(2 * count):
            if b < WIN:
                tail = pair_refs[b // 2][b % 2, 96:112, 0:128].astype(f32)
                slots_ref[b : b + 1, :] = tail[0:1].astype(jnp.int32)
            for j in range(KB):
                x = pair_refs[b // 2][b % 2, 16 * j : 16 * j + 16, :].astype(f32)
                if b < WIN:
                    left[b * KB + j] = x
                if b > 0:
                    index = (b - 1) * 3 + j // 2
                    for r in range(2):
                        half = x[8 * r : 8 * r + 8]
                        turned = pltpu.roll(half, 4, 0)
                        if j % 2 == 0:
                            right[index, 0, r] = half
                            right[index, 1, r] = turned
                        else:
                            right[index, 0, r] = jnp.where(low, right[index, 0, r], turned)
                            right[index, 1, r] = jnp.where(low, right[index, 1, r], half)
        together((), produce(0, va, ca))

    together(consume(0, va, ca), produce(2 * step + 1, vb, cb))
    together(consume(1, vb, cb), produce(jnp.minimum(2 * step + 2, 2 * steps - 1), va, ca))


def densities(pairs, zv, zc):
    whole = lambda shape: pl.BlockSpec(shape, lambda n: (0,) * len(shape), pipeline_mode=pl.Buffered(1))
    operands = list(pairs) + [zv, zc]
    in_specs = [whole(x.shape) for x in operands]
    count = len(pairs)
    steps = 3 * (count - 1)
    place = lambda n: (n, 0, 0)
    wv = zv.shape[1]
    wc = zc.shape[1]
    return pl.pallas_call(
        functools.partial(density_kernel, count, steps),
        grid=(steps,),
        in_specs=in_specs,
        out_specs=[
            pl.BlockSpec((48, 16, wv), place),
            pl.BlockSpec((48, 16, wc), place),
            pl.BlockSpec((WIN, 128), lambda n: (0, 0)),
        ],
        out_shape=[
            jax.ShapeDtypeStruct((TOTAL, 16, wv), bf16),
            jax.ShapeDtypeStruct((TOTAL, 16, wc), bf16),
            jax.ShapeDtypeStruct((WIN, 128), jnp.int32),
        ],
        scratch_shapes=[
            pltpu.VMEM((WIN * KB, 16, 1024), f32),
            pltpu.VMEM(((2 * count - 1) * 3, 2, 2, 8, 1024), f32),
            pltpu.VMEM((384, 2048), bf16),
            pltpu.VMEM((384, 2048), bf16),
            pltpu.VMEM((384, 2048), bf16),
            pltpu.VMEM((384, 2048), bf16),
        ],
        compiler_params=pltpu.CompilerParams(vmem_limit_bytes=VMEM_LIMIT),
        cost_estimate=pl.CostEstimate(
            flops=2 * steps * 48 * 16 * 2048 * (wv + wc), bytes_accessed=steps * 3 * 2**20, transcendentals=0
        ),
        name="densities",
    )(*operands)


def quarter_rows():
    own = [[(0, 0, 0, 16)], [(0, 16, 0, 8), (1, 0, 8, 8)], [(1, 8, 0, 16)]]
    own += [[(q + 2, r, s, n) for q, r, s, n in item] for item in own]
    mirror = [[(0, 24)], [(0, 40), (1, 24)], [(1, 40)]]
    mirror += [[(q + 2, r) for q, r in item] for item in mirror]
    return own, mirror


def apply_kernel(order_ref, slot_ref, used_ref, ga_ref, mv_hbm, mc_hbm, w_ref, out_ref, rhs, xv, mv_ref, mc_ref, done):
    fetch_v = pltpu.make_async_copy(mv_hbm, mv_ref, done.at[0])
    fetch_c = pltpu.make_async_copy(mc_hbm, mc_ref, done.at[1])
    fetch_v.start()
    ga = ga_ref[0]
    lane_group = lax.broadcasted_iota(jnp.int32, (16, 128), 1) >> 5
    spots = [(((q & 1) ^ (ga & 1)) << 1) | ((q >> 1) ^ (ga >> 1)) for q in range(4)]
    own_rows, mirror_rows = quarter_rows()

    def build(slot, carry):
        for x in range(4):
            wr = w_ref[x, slot, 0]
            wi = w_ref[x, slot, 1]
            rhs[slot, 64 * x : 64 * x + 64, 0:128] = wr
            rhs[slot, 64 * x : 64 * x + 64, 128:256] = -wi
            rhs[slot, 256 + 64 * x : 320 + 64 * x, 0:128] = wi
            rhs[slot, 256 + 64 * x : 320 + 64 * x, 128:256] = wr
        return carry

    lax.fori_loop(0, SLOTS, build, 0)
    fetch_v.wait()
    fetch_c.start()

    def chunk(q, carry):
        for u in range(UNROLL):
            slot = slot_ref[UNROLL * q + u]
            ids = [order_ref[(UNROLL * q + u) * CHUNK + i] for i in range(CHUNK)]
            sources = [jnp.minimum(i, TOTAL - 1) for i in ids]
            lhs = jnp.concatenate([mv_ref[s] for s in sources], axis=0)
            res = jnp.dot(lhs, rhs[slot], preferred_element_type=f32).astype(bf16)
            for i in range(CHUNK):
                xv[ids[i]] = res[16 * i : 16 * i + 16]
        return carry

    lax.fori_loop(0, (used_ref[0] + UNROLL - 1) >> 2, chunk, 0)
    fetch_c.wait()

    def contract(t, carry):
        for jh in range(3):
            for h in range(3):
                first = ((t * 3 + jh) * 6 + 2 * h) * 4
                rows = []
                for i in range(8):
                    y = mc_ref[first + i]
                    rows.append(y)
                    rows.append(jnp.concatenate([-y[:, 128:], y[:, :128]], axis=1))
                lhs = jnp.concatenate([xv[first + i] for i in range(8)], axis=0)
                d = lax.dot_general(
                    lhs, jnp.concatenate(rows, axis=0), (((1,), (1,)), ((), ())), preferred_element_type=f32
                )
                blocks = [
                    [d[16 * i : 16 * i + 16, 128 * (i // 4) : 128 * (i // 4) + 128] for i in range(4 * l, 4 * l + 4)]
                    for l in range(2)
                ]
                odd = (lane_group & 1) == 1
                low = lane_group < 2
                mixed = [[jnp.where(odd, b[2 * jl + 1], b[2 * jl]) for jl in range(2)] for b in blocks]
                for l in range(2):
                    own = jnp.where(low, mixed[l][0], mixed[l][1])
                    for q, r, s, n in own_rows[2 * h + l]:
                        out_ref[spots[q], t, jh, r : r + n, :] = own[s : s + n]
                for jl in range(2):
                    if jl == 0:
                        mirror = jnp.where(low, mixed[0][0], pltpu.roll(mixed[1][0], 64, 1))
                    else:
                        mirror = jnp.where(low, pltpu.roll(mixed[0][1], 64, 1), mixed[1][1])
                    for q, r in mirror_rows[2 * jh + jl]:
                        out_ref[spots[q], t, h, r : r + 16, :] = mirror
        return carry

    lax.fori_loop(0, WIN, contract, 0)


def apply_screened(order, slots, used, ga, mv, mc, w):
    smem = pl.BlockSpec(memory_space=pltpu.SMEM)
    vmem = pl.BlockSpec(memory_space=pltpu.VMEM)
    return pl.pallas_call(
        apply_kernel,
        in_specs=[smem] * 4 + [pl.BlockSpec(memory_space=pl.ANY)] * 2 + [vmem],
        out_specs=vmem,
        out_shape=jax.ShapeDtypeStruct((4, WIN, 3, 56, 128), f32),
        scratch_shapes=[
            pltpu.VMEM((SLOTS, 512, 256), bf16),
            pltpu.VMEM((TOTAL + 1, 16, 256), bf16),
            pltpu.VMEM(mv.shape, bf16),
            pltpu.VMEM(mc.shape, bf16),
            pltpu.SemaphoreType.DMA((2,)),
        ],
        compiler_params=pltpu.CompilerParams(vmem_limit_bytes=VMEM_LIMIT),
        cost_estimate=pl.CostEstimate(flops=6 * 10**9, bytes_accessed=18 * 2**20, transcendentals=0),
        name="apply_screened",
    )(order, slots, used, ga, mv, mc, w)


def split_dot(x, sel):
    high = x.astype(bf16)
    low = (x - high.astype(f32)).astype(bf16)
    return jnp.dot(high, sel, preferred_element_type=f32) + jnp.dot(low, sel, preferred_element_type=f32)


def arrange_kernel(ga_ref, parts_ref, out_ref):
    ga = ga_ref[0]
    src = lax.broadcasted_iota(jnp.int32, (128, 384), 0)
    lane = lax.broadcasted_iota(jnp.int32, (128, 384), 1)
    row = lax.broadcasted_iota(jnp.int32, (32, 384), 0)
    row_lane = lax.broadcasted_iota(jnp.int32, (32, 384), 1)
    start = ga + (ga >> 1)
    outer = row_lane >> 6
    place = 6 * ga + outer
    own = (24, (lane >> 4) & 3, lane & 3, outer * 4 + ((row_lane >> 2) & 3))
    mirror = (32, lane & 3, (lane >> 4) & 3, ((place >> 2) - start) * 16 + ((row_lane >> 2) & 3) * 4 + (place & 3))
    for kind, (count, c, c2, wanted) in enumerate((own, mirror)):
        low = 24 * kind
        x = jnp.concatenate([parts_ref[jh, low : low + count, :] for jh in range(3)], axis=0)
        keep = row[:count] == wanted[:count]
        for combo in range(8):
            sel = (src == combo * 16 + c * 4 + c2).astype(f32).astype(bf16)
            spread = split_dot(x, sel)
            for jh in range(3):
                rows = spread[count * jh : count * jh + count]
                picked = jnp.sum(jnp.where(keep, rows, 0.0), axis=0, keepdims=True)
                if kind == 1 and combo % 2 == 1:
                    picked = -picked
                out_ref[2 * jh + combo // 4, 2 * kind + (combo // 2) % 2, pl.ds(combo % 2, 1), :] = picked


def arrange(ga, parts):
    vmem = pl.BlockSpec(memory_space=pltpu.VMEM)
    return pl.pallas_call(
        arrange_kernel,
        in_specs=[pl.BlockSpec(memory_space=pltpu.SMEM), vmem],
        out_specs=vmem,
        out_shape=jax.ShapeDtypeStruct((KB, 4, 2, 384), f32),
        compiler_params=pltpu.CompilerParams(vmem_limit_bytes=VMEM_LIMIT),
        name="arrange",
    )(ga, parts)


def schedule(slots):
    pair = jnp.arange(TOTAL, dtype=jnp.int32)
    names = jnp.arange(SLOTS, dtype=jnp.int32)
    hot = slots[:, None] == names[None, :]
    needed = (jnp.sum(hot.astype(jnp.int32), axis=0) + CHUNK - 1) // CHUNK
    start = jnp.sum(jnp.where(names[:, None] < names[None, :], needed[:, None], 0), axis=0)
    same = (slots[:, None] == slots[None, :]) & (pair[None, :] < pair[:, None])
    rank = jnp.sum(same.astype(jnp.int32), axis=1)
    place = jnp.sum(jnp.where(hot, start[None, :], 0), axis=1) * CHUNK + rank
    seat = jnp.arange(CHUNKS * CHUNK, dtype=jnp.int32)
    taken = place[None, :] == seat[:, None]
    order = TOTAL + jnp.sum(jnp.where(taken, pair[None, :] - TOTAL, 0), axis=1)
    chunk = jnp.arange(CHUNKS, dtype=jnp.int32)
    ended = (start + needed)[None, :] <= chunk[:, None]
    slot_of = jnp.minimum(jnp.sum(ended.astype(jnp.int32), axis=1), SLOTS - 1)
    return order, slot_of, jnp.sum(needed).reshape(1)


def zeta_matrix(zeta):
    zr = zeta[:, 0]
    zi = zeta[:, 1]
    return jnp.concatenate([jnp.concatenate([zr, zi], axis=1), jnp.concatenate([-zi, zr], axis=1)], axis=0)


def body(bloch_samples, zeta_vectors, screened, pair_slots):
    ka_count = lax.axis_size("ka")
    ka = lax.axis_index("ka")
    ga = lax.axis_index("ga")
    ga_word = ga.reshape(1).astype(jnp.int32)
    part = lax.rem(ka, WIN)
    slots = jnp.transpose(pair_slots.reshape(3, 2, 2, KB), (0, 3, 1, 2)).reshape(1, PAIRS)
    tail = jnp.pad(slots.astype(bf16), ((0, 15), (0, 1024 - PAIRS)))
    message = jnp.concatenate([bloch_samples.reshape(96, 1024), tail], axis=0)
    following = from_behind(message, "ka", -1)
    here = jnp.stack([message, following])
    ahead = from_behind(here, "ka", -2)
    behind = from_behind(here, "ka", 2)
    zv = zeta_matrix(zeta_vectors)
    mine = lax.dynamic_slice_in_dim(zeta_vectors, 128 * lax.rem(part, 2), 128, 2)
    halves = lax.all_gather(mine, "ga")
    zc = zeta_matrix(lax.dynamic_index_in_dim(halves, part // 2, 0, keepdims=False))
    pieces = jnp.transpose(screened.reshape(SLOTS, 2, 4, WIN, 128), (3, 0, 1, 2, 4))
    pieces = jnp.concatenate([pieces, pieces], axis=0)
    pieces = pieces + following[0, 0] * 0
    line = 2 * WIN
    near_groups = [[x * line + s for s in range(line)] for x in range(ka_count // line)]
    x_groups = [[x * line + s for x in range(ka_count // line)] for s in range(line)]
    pieces = lax.all_to_all(pieces, "ka", 0, 0, axis_index_groups=near_groups, tiled=True)
    rows = jnp.transpose(pieces, (1, 2, 0, 3, 4)).reshape(SLOTS, 2, 4 * line, 128)
    w = lax.all_gather(rows, "ka", axis_index_groups=x_groups)
    ahead2 = from_behind(ahead, "ka", -2)
    behind2 = from_behind(behind, "ka", 2)
    mv, mc, words = densities((behind2, behind, here, ahead, ahead2), zv, zc)
    order, slot_of, used = schedule(words[:, :PAIRS].reshape(TOTAL))
    partial = apply_screened(order, slot_of, used, ga_word, mv, mc, w)
    arrived = lax.ppermute(partial[2:].astype(bf16), "ga", [(0, 1), (1, 0), (2, 3), (3, 2)])
    own = partial[0] + arrived[0].astype(f32)
    other = (partial[1] + arrived[1].astype(f32)).astype(bf16)
    own = own + lax.ppermute(other, "ga", [(0, 2), (2, 0), (1, 3), (3, 1)]).astype(f32)
    first_offset = ((lax.broadcasted_iota(jnp.int32, (1, 1, 1, 128), 3) >> 5) & 1) == 0
    spread = lambda x, before, after: jnp.pad(x, ((before, after), (0, 0), (0, 0), (0, 0)))
    mirror = jnp.where(first_offset, spread(own[:, :, 24:], 1, 1), spread(own[:, :, 24:], 2, 0))
    parts = jnp.concatenate([spread(own[:, :, :24], 0, 2), mirror], axis=2)
    send = lambda picks, by: from_behind(jnp.stack([parts[d] for d in picks]).astype(bf16), "ka", by).astype(f32)
    plus_one = send((1, 5, 9), 1)
    plus_two = send((2, 6), 2)
    minus_one = send((3, 7), -1)
    low = parts[0] + plus_one[0] + plus_two[0]
    high = parts[8] + plus_one[2] + minus_one[1]
    total = parts[4] + plus_one[1] + plus_two[1] + minus_one[0]
    total = total + from_behind(low, "ka", -4) + from_behind(high, "ka", 4)
    return arrange(ga_word, total)


def solution(mesh):
    in_specs = (
        P("ka", None, None, None),
        P(None, None, "ga"),
        P(None, None, ("ga", "ka"), None),
        P("ka", None, None),
    )
    out_specs = P("ka", None, None, "ga")
    return jax.shard_map(body, mesh=mesh, in_specs=in_specs, out_specs=out_specs, check_vma=False)
```

```python
import functools
import jax
import jax.numpy as jnp
from jax import lax
from jax.experimental import pallas as pl
from jax.experimental.pallas import tpu as pltpu
from jax.sharding import PartitionSpec as P

f32 = jnp.float32
bf16 = jnp.bfloat16

WIN = 8
KB = 6
PAIRS = 72
TOTAL = WIN * PAIRS
CHUNK = 16
SLOTS = 22
UNROLL = 4
CHUNKS = (TOTAL + SLOTS * (CHUNK - 1)) // CHUNK // UNROLL * UNROLL + UNROLL
MSG = 112
VMEM_LIMIT = 50 * 2**20


def from_behind(x, axis, by):
    count = lax.axis_size(axis)
    return lax.ppermute(x, axis, [(i, (i + by) % count) for i in range(count)])


def half_swap(mask, first, second):
    return jnp.where(mask, first, pltpu.roll(second, 4, 0))


def density_kernel(count, steps, *refs):
    pair_refs = refs[:count]
    zv_ref, zc_ref = refs[count : count + 2]
    mv_ref, mc_ref, slots_ref, left, right, va, ca, vb, cb = refs[-9:]
    step = pl.program_id(0)
    low = lax.broadcasted_iota(jnp.int32, (8, 1024), 0) < 4

    def produce(chunk, v_buf, c_buf):
        block = chunk // 3
        jh = chunk % 3
        for cv, buf in ((0, v_buf), (1, c_buf)):
            for jl in range(2):
                point = block * KB + 2 * jh + jl
                for part in range(4):
                    cols = slice(256 * part, 256 * part + 256)
                    imag_cols = slice(1024 + 256 * part, 1280 + 256 * part)
                    lefts = []
                    for band in range(4):
                        row = 4 * cv + band
                        lr = jnp.broadcast_to(left[point, row : row + 1, cols], (8, 256))
                        li = jnp.broadcast_to(left[point, 8 + row : 9 + row, cols], (8, 256))
                        lefts.append((lr, li))
                    for o in range(2):
                        for p in range(3):
                            rr = right[(block + o) * 3 + p, cv, 0, :, cols]
                            ri = right[(block + o) * 3 + p, cv, 1, :, cols]
                            base = ((jl * 2 + o) * 3 + p) * 32
                            for half in range(2):
                                reals = []
                                imags = []
                                for lr, li in lefts[2 * half : 2 * half + 2]:
                                    reals.append(lr * rr + li * ri)
                                    imags.append(lr * ri - li * rr)
                                rows = slice(base + 16 * half, base + 16 * half + 16)
                                buf[rows, cols] = jnp.concatenate(reals, axis=0).astype(bf16)
                                buf[rows, imag_cols] = jnp.concatenate(imags, axis=0).astype(bf16)
                    yield

    def consume(sub, v_buf, c_buf):
        mask = lax.broadcasted_iota(jnp.int32, (8, 256), 0) < 4
        for buf, z_ref, out_ref in ((v_buf, zv_ref, mv_ref), (c_buf, zc_ref, mc_ref)):
            for tile in range(z_ref.shape[1] // 256):
                cols = slice(256 * tile, 256 * tile + 256)
                res = jnp.dot(buf[...], z_ref[:, cols], preferred_element_type=f32)
                yield
                for group in range(12):
                    base = group * 32
                    jl, o, p = group // 6, group // 3 % 2, group % 3
                    a = [res[base + 8 * c : base + 8 * c + 8] for c in range(4)]
                    first = [half_swap(mask, a[0], a[1]), half_swap(mask, a[2], a[3])]
                    second = [
                        jnp.where(mask, pltpu.roll(a[0], 4, 0), a[1]),
                        jnp.where(mask, pltpu.roll(a[2], 4, 0), a[3]),
                    ]
                    for jj, value in ((0, first), (1, second)):
                        index = sub * 24 + (2 * p + jj) * 4 + jl * 2 + o
                        out_ref[index, :, cols] = jnp.concatenate(value, axis=0).astype(bf16)

    def together(matmuls, products):
        for _ in matmuls:
            for _ in range(6):
                next(products, None)
        for _ in products:
            pass

    @pl.when(step == 0)
    def _():
        for b in range(2 * count):
            if b < WIN:
                tail = pair_refs[b // 2][b % 2, 96:112, 0:128].astype(f32)
                slots_ref[b : b + 1, :] = tail[0:1].astype(jnp.int32)
            for j in range(KB):
                x = pair_refs[b // 2][b % 2, 16 * j : 16 * j + 16, :].astype(f32)
                if b < WIN:
                    left[b * KB + j] = x
                if b > 0:
                    index = (b - 1) * 3 + j // 2
                    for r in range(2):
                        half = x[8 * r : 8 * r + 8]
                        turned = pltpu.roll(half, 4, 0)
                        if j % 2 == 0:
                            right[index, 0, r] = half
                            right[index, 1, r] = turned
                        else:
                            right[index, 0, r] = jnp.where(low, right[index, 0, r], turned)
                            right[index, 1, r] = jnp.where(low, right[index, 1, r], half)
        together((), produce(0, va, ca))

    together(consume(0, va, ca), produce(2 * step + 1, vb, cb))
    together(consume(1, vb, cb), produce(jnp.minimum(2 * step + 2, 2 * steps - 1), va, ca))


def densities(pairs, zv, zc):
    whole = lambda shape: pl.BlockSpec(shape, lambda n: (0,) * len(shape), pipeline_mode=pl.Buffered(1))
    operands = list(pairs) + [zv, zc]
    in_specs = [whole(x.shape) for x in operands]
    count = len(pairs)
    steps = 3 * (count - 1)
    place = lambda n: (n, 0, 0)
    wv = zv.shape[1]
    wc = zc.shape[1]
    return pl.pallas_call(
        functools.partial(density_kernel, count, steps),
        grid=(steps,),
        in_specs=in_specs,
        out_specs=[
            pl.BlockSpec((48, 16, wv), place),
            pl.BlockSpec((48, 16, wc), place),
            pl.BlockSpec((WIN, 128), lambda n: (0, 0)),
        ],
        out_shape=[
            jax.ShapeDtypeStruct((TOTAL, 16, wv), bf16),
            jax.ShapeDtypeStruct((TOTAL, 16, wc), bf16),
            jax.ShapeDtypeStruct((WIN, 128), jnp.int32),
        ],
        scratch_shapes=[
            pltpu.VMEM((WIN * KB, 16, 1024), f32),
            pltpu.VMEM(((2 * count - 1) * 3, 2, 2, 8, 1024), f32),
            pltpu.VMEM((384, 2048), bf16),
            pltpu.VMEM((384, 2048), bf16),
            pltpu.VMEM((384, 2048), bf16),
            pltpu.VMEM((384, 2048), bf16),
        ],
        compiler_params=pltpu.CompilerParams(vmem_limit_bytes=VMEM_LIMIT),
        cost_estimate=pl.CostEstimate(
            flops=2 * steps * 48 * 16 * 2048 * (wv + wc), bytes_accessed=steps * 3 * 2**20, transcendentals=0
        ),
        name="densities",
    )(*operands)


def quarter_rows():
    own = [[(0, 0, 0, 16)], [(0, 16, 0, 8), (1, 0, 8, 8)], [(1, 8, 0, 16)]]
    own += [[(q + 2, r, s, n) for q, r, s, n in item] for item in own]
    mirror = [[(0, 24)], [(0, 40), (1, 24)], [(1, 40)]]
    mirror += [[(q + 2, r) for q, r in item] for item in mirror]
    return own, mirror


def apply_kernel(order_ref, slot_ref, used_ref, ga_ref, mv_hbm, mc_hbm, w_ref, out_ref, rhs, xv, mv_ref, mc_ref, done):
    fetch_v = pltpu.make_async_copy(mv_hbm, mv_ref, done.at[0])
    fetch_c = pltpu.make_async_copy(mc_hbm, mc_ref, done.at[1])
    fetch_v.start()
    ga = ga_ref[0]
    lane_group = lax.broadcasted_iota(jnp.int32, (16, 128), 1) >> 5
    spots = [(((q & 1) ^ (ga & 1)) << 1) | ((q >> 1) ^ (ga >> 1)) for q in range(4)]
    own_rows, mirror_rows = quarter_rows()

    def build(slot, carry):
        for x in range(4):
            wr = w_ref[x, slot, 0]
            wi = w_ref[x, slot, 1]
            rhs[slot, 64 * x : 64 * x + 64, 0:128] = wr
            rhs[slot, 64 * x : 64 * x + 64, 128:256] = -wi
            rhs[slot, 256 + 64 * x : 320 + 64 * x, 0:128] = wi
            rhs[slot, 256 + 64 * x : 320 + 64 * x, 128:256] = wr
        return carry

    lax.fori_loop(0, SLOTS, build, 0)
    fetch_v.wait()
    fetch_c.start()

    def chunk(q, carry):
        for u in range(UNROLL):
            slot = slot_ref[UNROLL * q + u]
            ids = [order_ref[(UNROLL * q + u) * CHUNK + i] for i in range(CHUNK)]
            sources = [jnp.minimum(i, TOTAL - 1) for i in ids]
            lhs = jnp.concatenate([mv_ref[s] for s in sources], axis=0)
            res = jnp.dot(lhs, rhs[slot], preferred_element_type=f32).astype(bf16)
            for i in range(CHUNK):
                xv[ids[i]] = res[16 * i : 16 * i + 16]
        return carry

    lax.fori_loop(0, (used_ref[0] + UNROLL - 1) >> 2, chunk, 0)
    fetch_c.wait()

    def contract(t, carry):
        for jh in range(3):
            for h in range(3):
                first = ((t * 3 + jh) * 6 + 2 * h) * 4
                rows = []
                for i in range(8):
                    y = mc_ref[first + i]
                    rows.append(y)
                    rows.append(jnp.concatenate([-y[:, 128:], y[:, :128]], axis=1))
                lhs = jnp.concatenate([xv[first + i] for i in range(8)], axis=0)
                d = lax.dot_general(
                    lhs, jnp.concatenate(rows, axis=0), (((1,), (1,)), ((), ())), preferred_element_type=f32
                )
                blocks = [
                    [d[16 * i : 16 * i + 16, 128 * (i // 4) : 128 * (i // 4) + 128] for i in range(4 * l, 4 * l + 4)]
                    for l in range(2)
                ]
                odd = (lane_group & 1) == 1
                low = lane_group < 2
                mixed = [[jnp.where(odd, b[2 * jl + 1], b[2 * jl]) for jl in range(2)] for b in blocks]
                for l in range(2):
                    own = jnp.where(low, mixed[l][0], mixed[l][1])
                    for q, r, s, n in own_rows[2 * h + l]:
                        out_ref[spots[q], t, jh, r : r + n, :] = own[s : s + n]
                for jl in range(2):
                    if jl == 0:
                        mirror = jnp.where(low, mixed[0][0], pltpu.roll(mixed[1][0], 64, 1))
                    else:
                        mirror = jnp.where(low, pltpu.roll(mixed[0][1], 64, 1), mixed[1][1])
                    for q, r in mirror_rows[2 * jh + jl]:
                        out_ref[spots[q], t, h, r : r + 16, :] = mirror
        return carry

    lax.fori_loop(0, WIN, contract, 0)


def apply_screened(order, slots, used, ga, mv, mc, w):
    smem = pl.BlockSpec(memory_space=pltpu.SMEM)
    vmem = pl.BlockSpec(memory_space=pltpu.VMEM)
    return pl.pallas_call(
        apply_kernel,
        in_specs=[smem] * 4 + [pl.BlockSpec(memory_space=pl.ANY)] * 2 + [vmem],
        out_specs=vmem,
        out_shape=jax.ShapeDtypeStruct((4, WIN, 3, 56, 128), f32),
        scratch_shapes=[
            pltpu.VMEM((SLOTS, 512, 256), bf16),
            pltpu.VMEM((TOTAL + 1, 16, 256), bf16),
            pltpu.VMEM(mv.shape, bf16),
            pltpu.VMEM(mc.shape, bf16),
            pltpu.SemaphoreType.DMA((2,)),
        ],
        compiler_params=pltpu.CompilerParams(vmem_limit_bytes=VMEM_LIMIT),
        cost_estimate=pl.CostEstimate(flops=6 * 10**9, bytes_accessed=18 * 2**20, transcendentals=0),
        name="apply_screened",
    )(order, slots, used, ga, mv, mc, w)


def split_dot(x, sel):
    high = x.astype(bf16)
    low = (x - high.astype(f32)).astype(bf16)
    return jnp.dot(high, sel, preferred_element_type=f32) + jnp.dot(low, sel, preferred_element_type=f32)


def arrange_kernel(ga_ref, parts_ref, out_ref):
    ga = ga_ref[0]
    src = lax.broadcasted_iota(jnp.int32, (128, 384), 0)
    lane = lax.broadcasted_iota(jnp.int32, (128, 384), 1)
    row = lax.broadcasted_iota(jnp.int32, (32, 384), 0)
    row_lane = lax.broadcasted_iota(jnp.int32, (32, 384), 1)
    start = ga + (ga >> 1)
    outer = row_lane >> 6
    place = 6 * ga + outer
    own = (24, (lane >> 4) & 3, lane & 3, outer * 4 + ((row_lane >> 2) & 3))
    mirror = (32, lane & 3, (lane >> 4) & 3, ((place >> 2) - start) * 16 + ((row_lane >> 2) & 3) * 4 + (place & 3))
    for kind, (count, c, c2, wanted) in enumerate((own, mirror)):
        low = 24 * kind
        x = jnp.concatenate([parts_ref[jh, low : low + count, :] for jh in range(3)], axis=0)
        keep = row[:count] == wanted[:count]
        for combo in range(8):
            sel = (src == combo * 16 + c * 4 + c2).astype(f32).astype(bf16)
            spread = split_dot(x, sel)
            for jh in range(3):
                rows = spread[count * jh : count * jh + count]
                picked = jnp.sum(jnp.where(keep, rows, 0.0), axis=0, keepdims=True)
                if kind == 1 and combo % 2 == 1:
                    picked = -picked
                out_ref[2 * jh + combo // 4, 2 * kind + (combo // 2) % 2, pl.ds(combo % 2, 1), :] = picked


def arrange(ga, parts):
    vmem = pl.BlockSpec(memory_space=pltpu.VMEM)
    return pl.pallas_call(
        arrange_kernel,
        in_specs=[pl.BlockSpec(memory_space=pltpu.SMEM), vmem],
        out_specs=vmem,
        out_shape=jax.ShapeDtypeStruct((KB, 4, 2, 384), f32),
        compiler_params=pltpu.CompilerParams(vmem_limit_bytes=VMEM_LIMIT),
        name="arrange",
    )(ga, parts)


def schedule(slots):
    pair = jnp.arange(TOTAL, dtype=jnp.int32)
    names = jnp.arange(SLOTS, dtype=jnp.int32)
    hot = slots[:, None] == names[None, :]
    needed = (jnp.sum(hot.astype(jnp.int32), axis=0) + CHUNK - 1) // CHUNK
    start = jnp.sum(jnp.where(names[:, None] < names[None, :], needed[:, None], 0), axis=0)
    same = (slots[:, None] == slots[None, :]) & (pair[None, :] < pair[:, None])
    rank = jnp.sum(same.astype(jnp.int32), axis=1)
    place = jnp.sum(jnp.where(hot, start[None, :], 0), axis=1) * CHUNK + rank
    seat = jnp.arange(CHUNKS * CHUNK, dtype=jnp.int32)
    taken = place[None, :] == seat[:, None]
    order = TOTAL + jnp.sum(jnp.where(taken, pair[None, :] - TOTAL, 0), axis=1)
    chunk = jnp.arange(CHUNKS, dtype=jnp.int32)
    ended = (start + needed)[None, :] <= chunk[:, None]
    slot_of = jnp.minimum(jnp.sum(ended.astype(jnp.int32), axis=1), SLOTS - 1)
    return order, slot_of, jnp.sum(needed).reshape(1)


def zeta_matrix(zeta):
    zr = zeta[:, 0]
    zi = zeta[:, 1]
    return jnp.concatenate([jnp.concatenate([zr, zi], axis=1), jnp.concatenate([-zi, zr], axis=1)], axis=0)


def body(bloch_samples, zeta_vectors, screened, pair_slots):
    ka_count = lax.axis_size("ka")
    ka = lax.axis_index("ka")
    ga = lax.axis_index("ga")
    ga_word = ga.reshape(1).astype(jnp.int32)
    part = lax.rem(ka, WIN)
    slots = jnp.transpose(pair_slots.reshape(3, 2, 2, KB), (0, 3, 1, 2)).reshape(1, PAIRS)
    tail = jnp.pad(slots.astype(bf16), ((0, 15), (0, 1024 - PAIRS)))
    message = jnp.concatenate([bloch_samples.reshape(96, 1024), tail], axis=0)
    following = from_behind(message, "ka", -1)
    here = jnp.stack([message, following])
    ahead = from_behind(here, "ka", -2)
    behind = from_behind(here, "ka", 2)
    zv = zeta_matrix(zeta_vectors)
    mine = lax.dynamic_slice_in_dim(zeta_vectors, 128 * lax.rem(part, 2), 128, 2)
    halves = lax.all_gather(mine, "ga")
    zc = zeta_matrix(lax.dynamic_index_in_dim(halves, part // 2, 0, keepdims=False))
    pieces = jnp.transpose(screened.reshape(SLOTS, 2, 4, WIN, 128), (3, 0, 1, 2, 4))
    pieces = jnp.concatenate([pieces, pieces], axis=0)
    pieces = pieces + (ahead[0, 0, 0] + behind[0, 0, 0]) * 0
    line = 2 * WIN
    near_groups = [[x * line + s for s in range(line)] for x in range(ka_count // line)]
    x_groups = [[x * line + s for x in range(ka_count // line)] for s in range(line)]
    pieces = lax.all_to_all(pieces, "ka", 0, 0, axis_index_groups=near_groups, tiled=True)
    rows = jnp.transpose(pieces, (1, 2, 0, 3, 4)).reshape(SLOTS, 2, 4 * line, 128)
    w = lax.all_gather(rows, "ka", axis_index_groups=x_groups)
    ahead2 = from_behind(ahead, "ka", -2)
    behind2 = from_behind(behind, "ka", 2)
    mv, mc, words = densities((behind2, behind, here, ahead, ahead2), zv, zc)
    order, slot_of, used = schedule(words[:, :PAIRS].reshape(TOTAL))
    partial = apply_screened(order, slot_of, used, ga_word, mv, mc, w)
    arrived = lax.ppermute(partial[2:].astype(bf16), "ga", [(0, 1), (1, 0), (2, 3), (3, 2)])
    own = partial[0] + arrived[0].astype(f32)
    other = (partial[1] + arrived[1].astype(f32)).astype(bf16)
    own = own + lax.ppermute(other, "ga", [(0, 2), (2, 0), (1, 3), (3, 1)]).astype(f32)
    first_offset = ((lax.broadcasted_iota(jnp.int32, (1, 1, 1, 128), 3) >> 5) & 1) == 0
    spread = lambda x, before, after: jnp.pad(x, ((before, after), (0, 0), (0, 0), (0, 0)))
    mirror = jnp.where(first_offset, spread(own[:, :, 24:], 1, 1), spread(own[:, :, 24:], 2, 0))
    parts = jnp.concatenate([spread(own[:, :, :24], 0, 2), mirror], axis=2)
    send = lambda picks, by: from_behind(jnp.stack([parts[d] for d in picks]).astype(bf16), "ka", by).astype(f32)
    plus_one = send((1, 5, 9), 1)
    plus_two = send((2, 6), 2)
    minus_one = send((3, 7), -1)
    low = parts[0] + plus_one[0] + plus_two[0]
    high = parts[8] + plus_one[2] + minus_one[1]
    total = parts[4] + plus_one[1] + plus_two[1] + minus_one[0]
    total = total + from_behind(low.astype(bf16), "ka", -4).astype(f32) + from_behind(high.astype(bf16), "ka", 4).astype(f32)
    return arrange(ga_word, total)


def solution(mesh):
    in_specs = (
        P("ka", None, None, None),
        P(None, None, "ga"),
        P(None, None, ("ga", "ka"), None),
        P("ka", None, None),
    )
    out_specs = P("ka", None, None, "ga")
    return jax.shard_map(body, mesh=mesh, in_specs=in_specs, out_specs=out_specs, check_vma=False)
```

```python
import functools
import jax
import jax.numpy as jnp
from jax import lax
from jax.experimental import pallas as pl
from jax.experimental.pallas import tpu as pltpu
from jax.sharding import PartitionSpec as P

f32 = jnp.float32
bf16 = jnp.bfloat16

WIN = 8
KB = 6
PAIRS = 72
TOTAL = WIN * PAIRS
CHUNK = 16
SLOTS = 22
UNROLL = 4
CHUNKS = (TOTAL + SLOTS * (CHUNK - 1)) // CHUNK // UNROLL * UNROLL + UNROLL
MSG = 112
VMEM_LIMIT = 50 * 2**20


def from_behind(x, axis, by):
    count = lax.axis_size(axis)
    return lax.ppermute(x, axis, [(i, (i + by) % count) for i in range(count)])


def half_swap(mask, first, second):
    return jnp.where(mask, first, pltpu.roll(second, 4, 0))


def density_kernel(count, rest, steps, *refs):
    pair_refs = refs[:count]
    zv_ref, zc_ref = refs[count : count + 2]
    mv_ref, mc_ref, slots_ref, left, right, va, ca, vb, cb = refs[-9:]
    step = pl.program_id(0)
    low = lax.broadcasted_iota(jnp.int32, (8, 1024), 0) < 4

    def produce(chunk, v_buf, c_buf):
        block = chunk // 3
        jh = chunk % 3
        if rest:
            block = block + jnp.where(block >= 2, 4, 0)
        for cv, buf in ((0, v_buf), (1, c_buf)):
            for jl in range(2):
                point = block * KB + 2 * jh + jl
                for part in range(4):
                    cols = slice(256 * part, 256 * part + 256)
                    imag_cols = slice(1024 + 256 * part, 1280 + 256 * part)
                    lefts = []
                    for band in range(4):
                        row = 4 * cv + band
                        lr = jnp.broadcast_to(left[point, row : row + 1, cols], (8, 256))
                        li = jnp.broadcast_to(left[point, 8 + row : 9 + row, cols], (8, 256))
                        lefts.append((lr, li))
                    for o in range(2):
                        for p in range(3):
                            rr = right[(block + o) * 3 + p, cv, 0, :, cols]
                            ri = right[(block + o) * 3 + p, cv, 1, :, cols]
                            base = ((jl * 2 + o) * 3 + p) * 32
                            for half in range(2):
                                reals = []
                                imags = []
                                for lr, li in lefts[2 * half : 2 * half + 2]:
                                    reals.append(lr * rr + li * ri)
                                    imags.append(lr * ri - li * rr)
                                rows = slice(base + 16 * half, base + 16 * half + 16)
                                buf[rows, cols] = jnp.concatenate(reals, axis=0).astype(bf16)
                                buf[rows, imag_cols] = jnp.concatenate(imags, axis=0).astype(bf16)
                    yield

    def consume(sub, v_buf, c_buf):
        mask = lax.broadcasted_iota(jnp.int32, (8, 256), 0) < 4
        for buf, z_ref, out_ref in ((v_buf, zv_ref, mv_ref), (c_buf, zc_ref, mc_ref)):
            for tile in range(z_ref.shape[1] // 256):
                cols = slice(256 * tile, 256 * tile + 256)
                res = jnp.dot(buf[...], z_ref[:, cols], preferred_element_type=f32)
                yield
                for group in range(12):
                    base = group * 32
                    jl, o, p = group // 6, group // 3 % 2, group % 3
                    a = [res[base + 8 * c : base + 8 * c + 8] for c in range(4)]
                    first = [half_swap(mask, a[0], a[1]), half_swap(mask, a[2], a[3])]
                    second = [
                        jnp.where(mask, pltpu.roll(a[0], 4, 0), a[1]),
                        jnp.where(mask, pltpu.roll(a[2], 4, 0), a[3]),
                    ]
                    for jj, value in ((0, first), (1, second)):
                        index = sub * 24 + (2 * p + jj) * 4 + jl * 2 + o
                        out_ref[index, :, cols] = jnp.concatenate(value, axis=0).astype(bf16)

    def together(matmuls, products):
        for _ in matmuls:
            for _ in range(6):
                next(products, None)
        for _ in products:
            pass

    @pl.when(step == 0)
    def _():
        for b in range(2 * count):
            if b < WIN:
                tail = pair_refs[b // 2][b % 2, 96:112, 0:128].astype(f32)
                slots_ref[b : b + 1, :] = tail[0:1].astype(jnp.int32)
            for j in range(KB):
                x = pair_refs[b // 2][b % 2, 16 * j : 16 * j + 16, :].astype(f32)
                left[b * KB + j] = x
                if b > 0:
                    index = (b - 1) * 3 + j // 2
                    for r in range(2):
                        half = x[8 * r : 8 * r + 8]
                        turned = pltpu.roll(half, 4, 0)
                        if j % 2 == 0:
                            right[index, 0, r] = half
                            right[index, 1, r] = turned
                        else:
                            right[index, 0, r] = jnp.where(low, right[index, 0, r], turned)
                            right[index, 1, r] = jnp.where(low, right[index, 1, r], half)
        together((), produce(0, va, ca))

    together(consume(0, va, ca), produce(2 * step + 1, vb, cb))
    together(consume(1, vb, cb), produce(jnp.minimum(2 * step + 2, 2 * steps - 1), va, ca))


def densities(pairs, rest, zv, zc, previous):
    whole = lambda shape: pl.BlockSpec(shape, lambda n: (0,) * len(shape), pipeline_mode=pl.Buffered(1))
    operands = list(pairs) + [zv, zc]
    in_specs = [whole(x.shape) for x in operands]
    aliases = {}
    if previous is not None:
        aliases = {len(operands): 0, len(operands) + 1: 1}
        in_specs += [pl.BlockSpec(memory_space=pl.ANY)] * 2
        operands += list(previous)
    count = len(pairs)
    steps = 6
    place = (lambda n: (n + jnp.where(n >= 3, 6, 0), 0, 0)) if rest else (lambda n: (3 + n, 0, 0))
    wv = zv.shape[1]
    wc = zc.shape[1]
    return pl.pallas_call(
        functools.partial(density_kernel, count, rest, steps),
        grid=(steps,),
        in_specs=in_specs,
        out_specs=[
            pl.BlockSpec((48, 16, wv), place),
            pl.BlockSpec((48, 16, wc), place),
            pl.BlockSpec((min(2 * count, WIN), 128), lambda n: (0, 0)),
        ],
        out_shape=[
            jax.ShapeDtypeStruct((TOTAL, 16, wv), bf16),
            jax.ShapeDtypeStruct((TOTAL, 16, wc), bf16),
            jax.ShapeDtypeStruct((min(2 * count, WIN), 128), jnp.int32),
        ],
        scratch_shapes=[
            pltpu.VMEM((2 * count * KB, 16, 1024), f32),
            pltpu.VMEM(((2 * count - 1) * 3, 2, 2, 8, 1024), f32),
            pltpu.VMEM((384, 2048), bf16),
            pltpu.VMEM((384, 2048), bf16),
            pltpu.VMEM((384, 2048), bf16),
            pltpu.VMEM((384, 2048), bf16),
        ],
        input_output_aliases=aliases,
        compiler_params=pltpu.CompilerParams(vmem_limit_bytes=VMEM_LIMIT),
        cost_estimate=pl.CostEstimate(
            flops=2 * steps * 48 * 16 * 2048 * (wv + wc), bytes_accessed=steps * 3 * 2**20, transcendentals=0
        ),
        name="densities",
    )(*operands)


def quarter_rows():
    own = [[(0, 0, 0, 16)], [(0, 16, 0, 8), (1, 0, 8, 8)], [(1, 8, 0, 16)]]
    own += [[(q + 2, r, s, n) for q, r, s, n in item] for item in own]
    mirror = [[(0, 24)], [(0, 40), (1, 24)], [(1, 40)]]
    mirror += [[(q + 2, r) for q, r in item] for item in mirror]
    return own, mirror


def apply_kernel(order_ref, slot_ref, used_ref, ga_ref, mv_hbm, mc_hbm, w_ref, out_ref, rhs, xv, mv_ref, mc_ref, done):
    fetch_v = pltpu.make_async_copy(mv_hbm, mv_ref, done.at[0])
    fetch_c = pltpu.make_async_copy(mc_hbm, mc_ref, done.at[1])
    fetch_v.start()
    ga = ga_ref[0]
    lane_group = lax.broadcasted_iota(jnp.int32, (16, 128), 1) >> 5
    spots = [(((q & 1) ^ (ga & 1)) << 1) | ((q >> 1) ^ (ga >> 1)) for q in range(4)]
    own_rows, mirror_rows = quarter_rows()

    def build(slot, carry):
        for x in range(4):
            wr = w_ref[x, slot, 0]
            wi = w_ref[x, slot, 1]
            rhs[slot, 64 * x : 64 * x + 64, 0:128] = wr
            rhs[slot, 64 * x : 64 * x + 64, 128:256] = -wi
            rhs[slot, 256 + 64 * x : 320 + 64 * x, 0:128] = wi
            rhs[slot, 256 + 64 * x : 320 + 64 * x, 128:256] = wr
        return carry

    lax.fori_loop(0, SLOTS, build, 0)
    fetch_v.wait()
    fetch_c.start()

    def chunk(q, carry):
        for u in range(UNROLL):
            slot = slot_ref[UNROLL * q + u]
            ids = [order_ref[(UNROLL * q + u) * CHUNK + i] for i in range(CHUNK)]
            sources = [jnp.minimum(i, TOTAL - 1) for i in ids]
            lhs = jnp.concatenate([mv_ref[s] for s in sources], axis=0)
            res = jnp.dot(lhs, rhs[slot], preferred_element_type=f32).astype(bf16)
            for i in range(CHUNK):
                xv[ids[i]] = res[16 * i : 16 * i + 16]
        return carry

    lax.fori_loop(0, (used_ref[0] + UNROLL - 1) >> 2, chunk, 0)
    fetch_c.wait()

    def contract(t, carry):
        for jh in range(3):
            for h in range(3):
                first = ((t * 3 + jh) * 6 + 2 * h) * 4
                rows = []
                for i in range(8):
                    y = mc_ref[first + i]
                    rows.append(y)
                    rows.append(jnp.concatenate([-y[:, 128:], y[:, :128]], axis=1))
                lhs = jnp.concatenate([xv[first + i] for i in range(8)], axis=0)
                d = lax.dot_general(
                    lhs, jnp.concatenate(rows, axis=0), (((1,), (1,)), ((), ())), preferred_element_type=f32
                )
                blocks = [
                    [d[16 * i : 16 * i + 16, 128 * (i // 4) : 128 * (i // 4) + 128] for i in range(4 * l, 4 * l + 4)]
                    for l in range(2)
                ]
                odd = (lane_group & 1) == 1
                low = lane_group < 2
                mixed = [[jnp.where(odd, b[2 * jl + 1], b[2 * jl]) for jl in range(2)] for b in blocks]
                for l in range(2):
                    own = jnp.where(low, mixed[l][0], mixed[l][1])
                    for q, r, s, n in own_rows[2 * h + l]:
                        out_ref[spots[q], t, jh, r : r + n, :] = own[s : s + n]
                for jl in range(2):
                    if jl == 0:
                        mirror = jnp.where(low, mixed[0][0], pltpu.roll(mixed[1][0], 64, 1))
                    else:
                        mirror = jnp.where(low, pltpu.roll(mixed[0][1], 64, 1), mixed[1][1])
                    for q, r in mirror_rows[2 * jh + jl]:
                        out_ref[spots[q], t, h, r : r + 16, :] = mirror
        return carry

    lax.fori_loop(0, WIN, contract, 0)


def apply_screened(order, slots, used, ga, mv, mc, w):
    smem = pl.BlockSpec(memory_space=pltpu.SMEM)
    vmem = pl.BlockSpec(memory_space=pltpu.VMEM)
    return pl.pallas_call(
        apply_kernel,
        in_specs=[smem] * 4 + [pl.BlockSpec(memory_space=pl.ANY)] * 2 + [vmem],
        out_specs=vmem,
        out_shape=jax.ShapeDtypeStruct((4, WIN, 3, 56, 128), f32),
        scratch_shapes=[
            pltpu.VMEM((SLOTS, 512, 256), bf16),
            pltpu.VMEM((TOTAL + 1, 16, 256), bf16),
            pltpu.VMEM(mv.shape, bf16),
            pltpu.VMEM(mc.shape, bf16),
            pltpu.SemaphoreType.DMA((2,)),
        ],
        compiler_params=pltpu.CompilerParams(vmem_limit_bytes=VMEM_LIMIT),
        cost_estimate=pl.CostEstimate(flops=6 * 10**9, bytes_accessed=18 * 2**20, transcendentals=0),
        name="apply_screened",
    )(order, slots, used, ga, mv, mc, w)


def split_dot(x, sel):
    high = x.astype(bf16)
    low = (x - high.astype(f32)).astype(bf16)
    return jnp.dot(high, sel, preferred_element_type=f32) + jnp.dot(low, sel, preferred_element_type=f32)


def arrange_kernel(ga_ref, parts_ref, out_ref):
    ga = ga_ref[0]
    src = lax.broadcasted_iota(jnp.int32, (128, 384), 0)
    lane = lax.broadcasted_iota(jnp.int32, (128, 384), 1)
    row = lax.broadcasted_iota(jnp.int32, (32, 384), 0)
    row_lane = lax.broadcasted_iota(jnp.int32, (32, 384), 1)
    start = ga + (ga >> 1)
    outer = row_lane >> 6
    place = 6 * ga + outer
    own = (24, (lane >> 4) & 3, lane & 3, outer * 4 + ((row_lane >> 2) & 3))
    mirror = (32, lane & 3, (lane >> 4) & 3, ((place >> 2) - start) * 16 + ((row_lane >> 2) & 3) * 4 + (place & 3))
    for kind, (count, c, c2, wanted) in enumerate((own, mirror)):
        low = 24 * kind
        x = jnp.concatenate([parts_ref[jh, low : low + count, :] for jh in range(3)], axis=0)
        keep = row[:count] == wanted[:count]
        for combo in range(8):
            sel = (src == combo * 16 + c * 4 + c2).astype(f32).astype(bf16)
            spread = split_dot(x, sel)
            for jh in range(3):
                rows = spread[count * jh : count * jh + count]
                picked = jnp.sum(jnp.where(keep, rows, 0.0), axis=0, keepdims=True)
                if kind == 1 and combo % 2 == 1:
                    picked = -picked
                out_ref[2 * jh + combo // 4, 2 * kind + (combo // 2) % 2, pl.ds(combo % 2, 1), :] = picked


def arrange(ga, parts):
    vmem = pl.BlockSpec(memory_space=pltpu.VMEM)
    return pl.pallas_call(
        arrange_kernel,
        in_specs=[pl.BlockSpec(memory_space=pltpu.SMEM), vmem],
        out_specs=vmem,
        out_shape=jax.ShapeDtypeStruct((KB, 4, 2, 384), f32),
        compiler_params=pltpu.CompilerParams(vmem_limit_bytes=VMEM_LIMIT),
        name="arrange",
    )(ga, parts)


def schedule(slots):
    pair = jnp.arange(TOTAL, dtype=jnp.int32)
    names = jnp.arange(SLOTS, dtype=jnp.int32)
    hot = slots[:, None] == names[None, :]
    needed = (jnp.sum(hot.astype(jnp.int32), axis=0) + CHUNK - 1) // CHUNK
    start = jnp.sum(jnp.where(names[:, None] < names[None, :], needed[:, None], 0), axis=0)
    same = (slots[:, None] == slots[None, :]) & (pair[None, :] < pair[:, None])
    rank = jnp.sum(same.astype(jnp.int32), axis=1)
    place = jnp.sum(jnp.where(hot, start[None, :], 0), axis=1) * CHUNK + rank
    seat = jnp.arange(CHUNKS * CHUNK, dtype=jnp.int32)
    taken = place[None, :] == seat[:, None]
    order = TOTAL + jnp.sum(jnp.where(taken, pair[None, :] - TOTAL, 0), axis=1)
    chunk = jnp.arange(CHUNKS, dtype=jnp.int32)
    ended = (start + needed)[None, :] <= chunk[:, None]
    slot_of = jnp.minimum(jnp.sum(ended.astype(jnp.int32), axis=1), SLOTS - 1)
    return order, slot_of, jnp.sum(needed).reshape(1)


def zeta_matrix(zeta):
    zr = zeta[:, 0]
    zi = zeta[:, 1]
    return jnp.concatenate([jnp.concatenate([zr, zi], axis=1), jnp.concatenate([-zi, zr], axis=1)], axis=0)


def body(bloch_samples, zeta_vectors, screened, pair_slots):
    ka_count = lax.axis_size("ka")
    ka = lax.axis_index("ka")
    ga = lax.axis_index("ga")
    ga_word = ga.reshape(1).astype(jnp.int32)
    part = lax.rem(ka, WIN)
    slots = jnp.transpose(pair_slots.reshape(3, 2, 2, KB), (0, 3, 1, 2)).reshape(1, PAIRS)
    tail = jnp.pad(slots.astype(bf16), ((0, 15), (0, 1024 - PAIRS)))
    message = jnp.concatenate([bloch_samples.reshape(96, 1024), tail], axis=0)
    following = from_behind(message, "ka", -1)
    here = jnp.stack([message, following])
    ahead = from_behind(here, "ka", -2)
    behind = from_behind(here, "ka", 2)
    zv = zeta_matrix(zeta_vectors)
    mine = lax.dynamic_slice_in_dim(zeta_vectors, 128 * lax.rem(part, 2), 128, 2)
    halves = lax.all_gather(mine, "ga")
    zc = zeta_matrix(lax.dynamic_index_in_dim(halves, part // 2, 0, keepdims=False))
    pieces = jnp.transpose(screened.reshape(SLOTS, 2, 4, WIN, 128), (3, 0, 1, 2, 4))
    pieces = jnp.concatenate([pieces, pieces], axis=0)
    line = 2 * WIN
    near_groups = [[x * line + s for s in range(line)] for x in range(ka_count // line)]
    x_groups = [[x * line + s for x in range(ka_count // line)] for s in range(line)]
    pieces = lax.all_to_all(pieces, "ka", 0, 0, axis_index_groups=near_groups, tiled=True)
    rows = jnp.transpose(pieces, (1, 2, 0, 3, 4)).reshape(SLOTS, 2, 4 * line, 128)
    w = lax.all_gather(rows, "ka", axis_index_groups=x_groups)
    ahead2 = from_behind(ahead, "ka", -2)
    behind2 = from_behind(behind, "ka", 2)
    mv, mc, _ = densities((behind, here, ahead), False, zv, zc, None)
    mv, mc, words = densities((behind2, behind, here, ahead, ahead2), True, zv, zc, (mv, mc))
    order, slot_of, used = schedule(words[:, :PAIRS].reshape(TOTAL))
    partial = apply_screened(order, slot_of, used, ga_word, mv, mc, w)
    arrived = lax.ppermute(partial[2:].astype(bf16), "ga", [(0, 1), (1, 0), (2, 3), (3, 2)])
    own = partial[0] + arrived[0].astype(f32)
    other = (partial[1] + arrived[1].astype(f32)).astype(bf16)
    own = own + lax.ppermute(other, "ga", [(0, 2), (2, 0), (1, 3), (3, 1)]).astype(f32)
    first_offset = ((lax.broadcasted_iota(jnp.int32, (1, 1, 1, 128), 3) >> 5) & 1) == 0
    spread = lambda x, before, after: jnp.pad(x, ((before, after), (0, 0), (0, 0), (0, 0)))
    mirror = jnp.where(first_offset, spread(own[:, :, 24:], 1, 1), spread(own[:, :, 24:], 2, 0))
    parts = jnp.concatenate([spread(own[:, :, :24], 0, 2), mirror], axis=2)
    send = lambda picks, by: from_behind(jnp.stack([parts[d] for d in picks]).astype(bf16), "ka", by).astype(f32)
    plus_one = send((1, 5, 9), 1)
    plus_two = send((2, 6), 2)
    minus_one = send((3, 7), -1)
    low = parts[0] + plus_one[0] + plus_two[0]
    high = parts[8] + plus_one[2] + minus_one[1]
    total = parts[4] + plus_one[1] + plus_two[1] + minus_one[0]
    total = total + from_behind(low, "ka", -4) + from_behind(high, "ka", 4)
    return arrange(ga_word, total)


def solution(mesh):
    in_specs = (
        P("ka", None, None, None),
        P(None, None, "ga"),
        P(None, None, ("ga", "ka"), None),
        P("ka", None, None),
    )
    out_specs = P("ka", None, None, "ga")
    return jax.shard_map(body, mesh=mesh, in_specs=in_specs, out_specs=out_specs, check_vma=False)
```
